32 devices in a mesh: freq: 8 (over y, x, core), mode: 4 (over z).
Axes of the slice: x: 2, y: 2, z: 4, core: 2. Of those that a mesh axis runs over, the one named last changes fastest.
Arguments:
- excitation: bfloat16 [16, 2, 256, 2048], P(None, None, 'freq', 'mode'), may hold values from -6 to 6
- coupling: bfloat16 [3, 8, 2, 2048, 2048], P(None, 'freq', None, 'mode'), may hold values from -3 to 3, as said below
- wavenumber: float32 [256, 2048], P('freq', 'mode'), may hold values from 0.02 to 0.2
- mode_counts: int32 [256], P('freq'), may hold values from 128 to 2048, as said below
- seg_steps: int32 [3], replicated, may hold values from 8 to 64
- shapes: bfloat16 [8, 2048, 512], P('freq'), may hold values from -0.125 to 0.125
- spectrum: float32 [2, 256], P(None, 'freq'), may hold values from -6 to 6
Outputs:
- traces: float32 [16, 512, 4096], P('mode', 'freq')
The draws below stay inside these ranges and needn't reach their ends.
Inputs may be any that keep to these rules, and one draw needn't show every extreme that they name: `mode_counts`: each count is a multiple of 128; counts tend to rise with frequency; the first frequency has 128 modes and the last has all 2048. `coupling`: the real part of each matrix is near the identity on its diagonal; all entries are independent otherwise.
All inputs are finite; a program needn't handle non-finite values.
Results may differ from the reference program's by a relative error of at most 0.015.
Values may be sent and summed in bfloat16 or wider, within the bound.
A program may use at most 128 MiB of HBM per device.

```python
import math
import jax
import jax.numpy as jnp
from jax import lax

M = 2048
MODE_BLOCK = 128
SEG = 3
SRC = 16
R = 512
NT = 4096
FREQ_DEV = 32
BANDS = 8
NF = 256
K0 = 16


def draw_coupling(key, part):
    full_shape = (SEG, BANDS, 2, M, M)
    noise_key = jax.random.fold_in(jax.random.fold_in(key, 17), 0)
    noise_part = jax.random.normal(noise_key, full_shape, jnp.float32)
    diagonal = jnp.ones((SEG, BANDS, 1, M, 1), jnp.float32)
    real_only = (jnp.arange(2) == 0).astype(jnp.float32).reshape(1, 1, 2, 1, 1)
    identity = jnp.eye(M, dtype=jnp.float32)
    matrix = real_only * diagonal * identity + noise_part * (0.4 / math.sqrt(M))
    return matrix.astype(jnp.bfloat16)


def draw_mode_counts(key, part):
    blocks = M // MODE_BLOCK
    position = jnp.arange(NF, dtype=jnp.int32)
    rising = 1 + (blocks - 1) * position // max(NF - 1, 1)
    jitter = jax.random.randint(jax.random.fold_in(key, 29), (NF,), -1, 2, dtype=jnp.int32)
    counts = jnp.clip(rising + jitter, 1, blocks)
    counts = jnp.where(position == 0, 1, jnp.where(position == NF - 1, blocks, counts))
    return (counts * MODE_BLOCK).astype(jnp.int32)


def block_scale(rng, dims, pieces, low, largest):
    loudness, own = 1.0, jax.random.fold_in(rng, 6)
    for axis_at, shards_of in pieces:
        draws = jnp.exp(jax.random.uniform(jax.random.fold_in(own, axis_at), (shards_of,), jnp.float32, low / len(pieces), largest / len(pieces)))
        loudness = loudness * jnp.repeat(draws, dims[axis_at] // shards_of).reshape([-1 if axis == axis_at else 1 for axis in range(len(dims))])
    return loudness


def noise(key, extent, scale, reach, shards=(), kind=jnp.bfloat16):
    loudness = block_scale(key, extent, shards, -0.22, 0.18) if shards else 1.0
    entries = jax.random.normal(key, extent, jnp.float32) * scale * loudness
    return jnp.minimum(jnp.maximum(entries, -reach), reach).astype(kind)


def setup_inputs(seed: int = 0) -> dict:
    keys = jax.random.split(jax.random.key(seed), 8)
    return {
        "excitation": noise(keys[0], (SRC, 2, NF, M), 1.0, 6.0, ((2, 8), (3, 4))),
        "coupling": draw_coupling(jax.random.fold_in(keys[7], 71), 0),
        "wavenumber": jnp.clip(0.02 + 0.18 * jax.random.uniform(keys[2], (NF, M), jnp.float32) ** block_scale(keys[2], (NF, M), ((0, 8), (1, 4)), -0.2, 0.2), 0.02, 0.2),
        "mode_counts": draw_mode_counts(jax.random.fold_in(keys[7], 71), 0),
        "seg_steps": jax.random.randint(keys[4], (SEG,), 8, 65).astype(jnp.int32),
        "shapes": noise(keys[5], (BANDS, M, R), M ** -0.5, 0.125, ((0, 8),)),
        "spectrum": noise(keys[6], (2, NF), 1.0, 6.0, ((1, 8),), jnp.float32),
    }


def make_table(first_bin, count):
    freq_index = first_bin + jnp.arange(count, dtype=jnp.int32)
    sample = jnp.arange(NT, dtype=jnp.int32)
    phase_step = (freq_index[:, None] + K0) * sample[None, :] % NT
    angles = phase_step.astype(jnp.float32) * (2.0 * math.pi / NT)
    return jnp.stack([jnp.cos(angles), -jnp.sin(angles)], axis=0).astype(jnp.bfloat16)

def propagate_band(band, excitation, coupling, wavenumber, mode_counts, seg_steps, shapes, spectrum):
    lowest = (band * FREQ_DEV).astype(jnp.int32)
    source_part = lax.dynamic_slice_in_dim(excitation, lowest, FREQ_DEV, 2)
    phase_rate = lax.dynamic_slice_in_dim(wavenumber, lowest, FREQ_DEV, 0)
    counts = lax.dynamic_slice_in_dim(mode_counts, lowest, FREQ_DEV, 0)
    living = (jnp.arange(M, dtype=jnp.int32)[None, :] < counts[:, None]).astype(jnp.float32)
    amplitude = (source_part.astype(jnp.float32) * living).astype(jnp.bfloat16)
    for segment in range(SEG):
        matrix = lax.dynamic_index_in_dim(coupling[segment], band, 0, keepdims=False)
        stacked = matrix.reshape(2 * M, M)
        product = jnp.dot(amplitude.reshape(SRC * 2 * FREQ_DEV, M), stacked.T, preferred_element_type=jnp.float32)
        product = product.reshape(SRC, 2, FREQ_DEV, 2, M)
        coupled_real = product[:, 0, :, 0] - product[:, 1, :, 1]
        coupled_imaginary = product[:, 1, :, 0] + product[:, 0, :, 1]
        angles = phase_rate * seg_steps[segment].astype(jnp.float32)
        factor_real = living * jnp.cos(angles)
        factor_imaginary = living * jnp.sin(angles)
        amplitude = jnp.stack([coupled_real * factor_real - coupled_imaginary * factor_imaginary, coupled_real * factor_imaginary + coupled_imaginary * factor_real], axis=1).astype(jnp.bfloat16)
    mode_shapes = lax.dynamic_index_in_dim(shapes, band, 0, keepdims=False)
    field = jnp.dot(amplitude.reshape(SRC * 2 * FREQ_DEV, M), mode_shapes, preferred_element_type=jnp.float32)
    field = field.reshape(SRC, 2, FREQ_DEV, R)
    weights = lax.dynamic_slice_in_dim(spectrum, lowest, FREQ_DEV, 1)
    weight_real = weights[0][None, :, None]
    weight_imaginary = weights[1][None, :, None]
    weighted = jnp.stack([weight_real * field[:, 0] - weight_imaginary * field[:, 1], weight_real * field[:, 1] + weight_imaginary * field[:, 0]], axis=1)
    return weighted.astype(jnp.bfloat16)

def reference(excitation, coupling, wavenumber, mode_counts, seg_steps, shapes, spectrum):

    def one_band(band):
        return propagate_band(band, excitation, coupling, wavenumber, mode_counts, seg_steps, shapes, spectrum)
    every_band = lax.map(one_band, jnp.arange(BANDS, dtype=jnp.int32))
    weighted = jnp.transpose(every_band, (1, 2, 0, 3, 4)).reshape(SRC, 2, NF, R)
    table = make_table(0, NF)
    summed = jnp.einsum('scfr,cft->srt', weighted.astype(jnp.float32), table.astype(jnp.float32))
    return summed * (1.0 / math.sqrt(NF))
```

```python
import functools
import math

import jax
import jax.numpy as jnp
from jax import lax
from jax.experimental import pallas as pl
from jax.experimental.pallas import tpu as pltpu
from jax.sharding import PartitionSpec as P

NT = 4096
LANES = 128


def propagate(
    n, nf, offset_bin, exc, coupling, wavenumber, counts, steps, shapes, weights,
    table, received,
    matrix, amp, factor, weighted, landed,
    load_sem, send_sem, recv_sem, own_send, own_recv, out_send, out_recv,
):
    segments = coupling.shape[0]
    sources, _, bins, modes = exc.shape
    cs = sources // n
    half = cs * bins
    receivers = shapes.shape[-1]
    rh = receivers // nf
    phases = segments * n
    me = lax.axis_index("mode")
    band = lax.axis_index("freq")

    def load(g):
        return pltpu.make_async_copy(coupling.at[g, 0], matrix.at[g], load_sem.at[g])

    def hop(g, k, sign, d):
        shard = me - sign * d
        way = (sign + 1) // 2
        return pltpu.make_async_remote_copy(
            src_ref=amp.at[g, k, shard],
            dst_ref=amp.at[g, k, shard],
            send_sem=send_sem.at[g, k, way, d],
            recv_sem=recv_sem.at[g, k, way, d],
            device_id={"mode": me + sign},
            device_id_type=pl.DeviceIdType.MESH,
        )

    def arrival(g, k, sign, d):
        shard = me - sign * (d + 1)
        way = (sign + 1) // 2
        return pltpu.make_async_remote_copy(
            src_ref=amp.at[g, k, shard],
            dst_ref=amp.at[g, k, shard],
            send_sem=send_sem.at[g, k, way, d],
            recv_sem=recv_sem.at[g, k, way, d],
            device_id={"mode": me - sign},
            device_id_type=pl.DeviceIdType.MESH,
        )

    def inside(z):
        return jnp.logical_and(z >= 0, z < n)

    lead = jnp.where(me < n // 2, -1, 1)

    def send_own(g, k):
        for sign in (lead, -lead):
            @pl.when(inside(me + sign))
            def _(sign=sign):
                hop(g, k, sign, 0).start()

    def to_owner(k):
        return pltpu.make_async_remote_copy(
            src_ref=amp.at[segments, k, me],
            dst_ref=amp.at[segments, k, me],
            send_sem=own_send.at[k],
            recv_sem=own_recv.at[me],
            device_id={"mode": k},
            device_id_type=pl.DeviceIdType.MESH,
        )

    for g in range(segments):
        load(g).start()

    barrier = pltpu.get_barrier_semaphore()

    @pl.loop(1, n)
    def _(i):
        pl.semaphore_signal(
            barrier, inc=1, device_id={"mode": lax.rem(me + i, n)},
            device_id_type=pl.DeviceIdType.MESH,
        )

    @pl.loop(1, nf)
    def _(i):
        pl.semaphore_signal(
            barrier, inc=1, device_id={"freq": lax.rem(band + i, nf)},
            device_id_type=pl.DeviceIdType.MESH,
        )

    mode_number = me * modes + lax.broadcasted_iota(jnp.int32, (bins, modes), 1)
    living = jnp.where(mode_number < counts[...], 1.0, 0.0).astype(jnp.float32)

    @pl.loop(0, n)
    def _(k):
        for c in range(2):
            x = exc[pl.ds(k * cs, cs), c].astype(jnp.float32) * living[None]
            amp[0, k, me, c * half:(c + 1) * half, :] = (
                x.reshape(half, modes).astype(jnp.bfloat16)
            )

    pl.semaphore_wait(barrier, n - 1 + nf - 1)
    send_own(0, 0)
    if n > 1:
        send_own(0, 1)

    for g in range(segments):
        angle = wavenumber[...] * steps[g].astype(jnp.float32)
        factor[g, 0] = living * jnp.cos(angle)
        factor[g, 1] = living * jnp.sin(angle)

    def table_block(j):
        f = j * bins + offset_bin + lax.broadcasted_iota(jnp.int32, (bins, LANES), 0)
        lane = lax.broadcasted_iota(jnp.int32, (bins, LANES), 1)
        unit = 2.0 * math.pi / NT
        fine = lax.rem(f * lane, NT).astype(jnp.float32) * unit
        coarse = lax.rem(f * (lane * LANES), NT).astype(jnp.float32) * unit
        cos_fine, sin_fine = jnp.cos(fine), jnp.sin(fine)
        cos_coarse, sin_coarse = jnp.cos(coarse), jnp.sin(coarse)
        row = pl.multiple_of(j * (2 * bins), 2 * bins)
        for a in range(NT // LANES):
            ca = cos_coarse[:, a:a + 1]
            sa = sin_coarse[:, a:a + 1]
            at = slice(a * LANES, (a + 1) * LANES)
            table[pl.ds(row, bins), at] = (ca * cos_fine - sa * sin_fine).astype(jnp.bfloat16)
            table[pl.ds(row + bins, bins), at] = (
                -(sa * cos_fine + ca * sin_fine)
            ).astype(jnp.bfloat16)

    width = min(256, modes)

    @pl.loop(0, phases)
    def _(p):
        g = p // n
        k = lax.rem(p, n)

        @pl.when(jnp.logical_and(g == 0, k + 2 < n))
        def _():
            send_own(0, k + 2)

        for d in range(n - 1):
            for sign in (lead, -lead):
                @pl.when(inside(me - sign * (d + 1)))
                def _(sign=sign, d=d):
                    arrival(g, k, sign, d).wait_recv()
                    if d + 1 < n - 1:
                        @pl.when(inside(me + sign))
                        def _():
                            hop(g, k, sign, d + 1).start()

        @pl.when(k == 0)
        def _():
            load(g).wait()

        @pl.loop(0, modes // width)
        def _(tile):
            rows = pl.ds(pl.multiple_of(tile * width, width), width)
            by_real = jnp.zeros((2 * half, width), jnp.float32)
            by_imag = jnp.zeros((2 * half, width), jnp.float32)
            for z in range(n):
                a = amp[g, k, z]
                cols = slice(z * modes, (z + 1) * modes)
                dims = (((1,), (1,)), ((), ()))
                by_real += lax.dot_general(
                    a, matrix[g, 0, rows, cols], dims, preferred_element_type=jnp.float32
                )
                by_imag += lax.dot_general(
                    a, matrix[g, 1, rows, cols], dims, preferred_element_type=jnp.float32
                )
            real = (by_real[:half] - by_imag[half:]).reshape(cs, bins, width)
            imag = (by_real[half:] + by_imag[:half]).reshape(cs, bins, width)
            fr = factor[g, 0, :, rows][None]
            fi = factor[g, 1, :, rows][None]
            amp[g + 1, k, me, 0:half, rows] = (
                (real * fr - imag * fi).reshape(half, width).astype(jnp.bfloat16)
            )
            amp[g + 1, k, me, half:2 * half, rows] = (
                (real * fi + imag * fr).reshape(half, width).astype(jnp.bfloat16)
            )

        @pl.when(g + 1 < segments)
        def _():
            send_own(g + 1, k)

        @pl.when(jnp.logical_and(g + 1 == segments, k != me))
        def _():
            to_owner(k).start()

        @pl.loop(0, (nf - p + phases - 1) // phases)
        def _(i):
            table_block(p + i * phases)

    @pl.loop(1, n)
    def _(i):
        z = lax.rem(me + i, n)
        pltpu.make_async_remote_copy(
            src_ref=amp.at[segments, me, z],
            dst_ref=amp.at[segments, me, z],
            send_sem=own_send.at[z],
            recv_sem=own_recv.at[z],
            device_id={"mode": z},
            device_id_type=pl.DeviceIdType.MESH,
        ).wait_recv()

    field = jnp.zeros((2 * half, receivers), jnp.float32)
    for z in range(n):
        field += jnp.dot(
            amp[segments, me, z], shapes[0, z * modes:(z + 1) * modes, :],
            preferred_element_type=jnp.float32,
        )
    wr, wi = weights[:, 0:1], weights[:, 1:2]
    fr, fi = field[:half], field[half:]
    weighted[0] = (wr * fr - wi * fi).T.astype(jnp.bfloat16)
    weighted[1] = (wr * fi + wi * fr).T.astype(jnp.bfloat16)

    def to_receiver(j, slot):
        return pltpu.make_async_remote_copy(
            src_ref=weighted.at[:, pl.ds(pl.multiple_of(j * rh, rh), rh)],
            dst_ref=landed.at[slot],
            send_sem=out_send.at[j],
            recv_sem=out_recv.at[slot],
            device_id={"freq": j},
            device_id_type=pl.DeviceIdType.MESH,
        )

    @pl.loop(1, nf)
    def _(i):
        to_receiver(lax.rem(band + i, nf), band).start()

    received[band] = weighted[:, pl.ds(pl.multiple_of(band * rh, rh), rh), :]

    @pl.loop(1, nf)
    def _(i):
        j = lax.rem(band + i, nf)
        to_receiver(j, j).wait_recv()
        received[j] = landed[j]

    @pl.loop(1, nf)
    def _(i):
        to_receiver(lax.rem(band + i, nf), band).wait_send()

    @pl.loop(0, phases)
    def _(p):
        g = p // n
        k = lax.rem(p, n)
        for d in range(n - 1):
            for sign in (lead, -lead):
                @pl.when(jnp.logical_and(inside(me - sign * d), inside(me + sign)))
                def _(sign=sign, d=d):
                    hop(g, k, sign, d).wait_send()

    @pl.loop(1, n)
    def _(i):
        to_owner(lax.rem(me + i, n)).wait_send()


def shards(excitation, coupling, wavenumber, mode_counts, seg_steps, shapes, spectrum):
    n = lax.axis_size("mode")
    nf = lax.axis_size("freq")
    sources, _, bins, modes = excitation.shape
    segments, _, _, _, all_modes = coupling.shape
    receivers = shapes.shape[-1]
    cs = sources // n
    half = cs * bins
    rh = receivers // nf
    all_bins = bins * nf
    vmem = pl.BlockSpec(memory_space=pltpu.VMEM)
    dma = pltpu.SemaphoreType.DMA
    table, received = pl.pallas_call(
        functools.partial(propagate, n, nf, all_bins // 16),
        out_shape=(
            jax.ShapeDtypeStruct((nf * 2 * bins, NT), jnp.bfloat16),
            jax.ShapeDtypeStruct((nf, 2, rh, half), jnp.bfloat16),
        ),
        in_specs=[
            vmem, pl.BlockSpec(memory_space=pl.ANY), vmem, vmem,
            pl.BlockSpec(memory_space=pltpu.SMEM), vmem, vmem,
        ],
        out_specs=(vmem, vmem),
        scratch_shapes=[
            pltpu.VMEM((segments, 2, modes, all_modes), jnp.bfloat16),
            pltpu.VMEM((segments + 1, n, n, 2 * half, modes), jnp.bfloat16),
            pltpu.VMEM((segments, 2, bins, modes), jnp.float32),
            pltpu.VMEM((2, receivers, half), jnp.bfloat16),
            pltpu.VMEM((nf, 2, rh, half), jnp.bfloat16),
            dma((segments,)),
            dma((segments, n, 2, n - 1)),
            dma((segments, n, 2, n - 1)),
            dma((n,)),
            dma((n,)),
            dma((nf,)),
            dma((nf,)),
        ],
        compiler_params=pltpu.CompilerParams(
            collective_id=0, has_side_effects=True, vmem_limit_bytes=60 * 1024 * 1024
        ),
        name="propagate",
    )(
        excitation, coupling, wavenumber, mode_counts.reshape(bins, 1), seg_steps, shapes,
        jnp.tile(spectrum.T, (cs, 1)),
    )
    left = received.reshape(nf, 2, rh, cs, bins).transpose(3, 2, 0, 1, 4)
    left = left.reshape(cs, rh, nf * 2 * bins)
    summed = lax.dot_general(
        left, table, (((2,), (0,)), ((), ())), preferred_element_type=jnp.float32
    )
    return summed * (1.0 / math.sqrt(all_bins))


def solution(mesh):
    in_specs = (
        P(None, None, "freq", "mode"),
        P(None, "freq", None, "mode", None),
        P("freq", "mode"),
        P("freq"),
        P(),
        P("freq", None, None),
        P(None, "freq"),
    )
    out_specs = P("mode", "freq", None)
    return jax.shard_map(shards, mesh=mesh, in_specs=in_specs, out_specs=out_specs, check_vma=False)
```

```python
import functools
import math

import jax
import jax.numpy as jnp
from jax import lax
from jax.experimental import pallas as pl
from jax.experimental.pallas import tpu as pltpu
from jax.sharding import PartitionSpec as P

NT = 4096
LANES = 128


def phase_order(segments, n):
    pairs = [(g, position) for g in range(segments) for position in range(n)]
    return sorted(pairs, key=lambda pair: (pair[1] + pair[0] * 0.625 * n, pair[0]))


def propagate(
    n, nf, offset_bin, exc, coupling, wavenumber, counts, steps, shapes, weights,
    table, received,
    matrix, amp, factor, weighted, landed, lent, lent_factor,
    load_sem, send_sem, recv_sem, own_send, own_recv, out_send, out_recv,
    lend_send, lend_recv, lend_factor_sem,
):
    segments = coupling.shape[0]
    sources, _, bins, modes = exc.shape
    cs = sources // n
    half = cs * bins
    receivers = shapes.shape[-1]
    rh = receivers // nf
    phases = segments * n
    me = lax.axis_index("mode")
    band = lax.axis_index("freq")

    relieve = n >= 4 and segments >= 2
    last = segments - 1
    order = phase_order(segments, n)
    first_last = [g for g, _ in order].index(last)
    lending = max(first_last - 1, 1)
    pieces = max(last, 1) * n
    piece = modes // pieces

    def at_end(z):
        return jnp.logical_and(relieve, jnp.logical_or(z == 0, z == n - 1))

    edge = at_end(me)
    helper = jnp.logical_and(relieve, jnp.logical_or(me == 1, me == n - 2))
    partner = jnp.where(me == 1, 0, n - 1)
    inward = jnp.where(me == 0, min(1, n - 1), max(n - 2, 0))

    def owner(position):
        return jnp.where(
            lax.rem(position, 2) == 0, position // 2, n - 1 - position // 2
        )

    def phase(p):
        g, position = jnp.int32(0), jnp.int32(0)
        for i, (at_g, at_position) in enumerate(order):
            g = jnp.where(p == i, at_g, g)
            position = jnp.where(p == i, at_position, position)
        return g, position

    def lend(q):
        rows = pl.ds(pl.multiple_of(q * piece, piece), piece)
        return pltpu.make_async_remote_copy(
            src_ref=matrix.at[last, :, rows],
            dst_ref=lent.at[:, rows],
            send_sem=lend_send.at[q],
            recv_sem=lend_recv.at[q],
            device_id={"mode": inward},
            device_id_type=pl.DeviceIdType.MESH,
        )

    def lend_factor():
        return pltpu.make_async_remote_copy(
            src_ref=factor.at[last],
            dst_ref=lent_factor,
            send_sem=lend_factor_sem.at[0],
            recv_sem=lend_factor_sem.at[1],
            device_id={"mode": inward},
            device_id_type=pl.DeviceIdType.MESH,
        )

    def load(g):
        return pltpu.make_async_copy(coupling.at[g, 0], matrix.at[g], load_sem.at[g])

    def hop(g, k, sign, d):
        shard = me - sign * d
        way = (sign + 1) // 2
        return pltpu.make_async_remote_copy(
            src_ref=amp.at[g, k, shard],
            dst_ref=amp.at[g, k, shard],
            send_sem=send_sem.at[g, k, way, d],
            recv_sem=recv_sem.at[g, k, way, d],
            device_id={"mode": me + sign},
            device_id_type=pl.DeviceIdType.MESH,
        )

    def arrival(g, k, sign, d):
        shard = me - sign * (d + 1)
        way = (sign + 1) // 2
        return pltpu.make_async_remote_copy(
            src_ref=amp.at[g, k, shard],
            dst_ref=amp.at[g, k, shard],
            send_sem=send_sem.at[g, k, way, d],
            recv_sem=recv_sem.at[g, k, way, d],
            device_id={"mode": me - sign},
            device_id_type=pl.DeviceIdType.MESH,
        )

    def inside(z):
        return jnp.logical_and(z >= 0, z < n)

    lead = jnp.where(me < n // 2, -1, 1)

    def wanted(g, z):
        return jnp.logical_and(inside(z), jnp.logical_not(jnp.logical_and(g == last, at_end(z))))

    def send_own(g, k):
        for sign in (lead, -lead):
            @pl.when(wanted(g, me + sign))
            def _(sign=sign):
                hop(g, k, sign, 0).start()

    def to_owner(k, shard, which):
        return pltpu.make_async_remote_copy(
            src_ref=amp.at[segments, k, shard],
            dst_ref=amp.at[segments, k, shard],
            send_sem=own_send.at[k, which],
            recv_sem=own_recv.at[shard],
            device_id={"mode": k},
            device_id_type=pl.DeviceIdType.MESH,
        )

    for g in range(segments):
        load(g).start()

    barrier = pltpu.get_barrier_semaphore()

    @pl.loop(1, n)
    def _(i):
        pl.semaphore_signal(
            barrier, inc=1, device_id={"mode": lax.rem(me + i, n)},
            device_id_type=pl.DeviceIdType.MESH,
        )

    @pl.loop(1, nf)
    def _(i):
        pl.semaphore_signal(
            barrier, inc=1, device_id={"freq": lax.rem(band + i, nf)},
            device_id_type=pl.DeviceIdType.MESH,
        )

    mode_number = me * modes + lax.broadcasted_iota(jnp.int32, (bins, modes), 1)
    living = jnp.where(mode_number < counts[...], 1.0, 0.0).astype(jnp.float32)

    @pl.loop(0, n)
    def _(k):
        for c in range(2):
            x = exc[pl.ds(k * cs, cs), c].astype(jnp.float32) * living[None]
            amp[0, k, me, c * half:(c + 1) * half, :] = (
                x.reshape(half, modes).astype(jnp.bfloat16)
            )

    pl.semaphore_wait(barrier, n - 1 + nf - 1)
    send_own(0, owner(jnp.int32(0)))
    if n > 1:
        send_own(0, owner(jnp.int32(1)))

    for g in range(segments):
        angle = wavenumber[...] * steps[g].astype(jnp.float32)
        factor[g, 0] = living * jnp.cos(angle)
        factor[g, 1] = living * jnp.sin(angle)

    @pl.when(edge)
    def _():
        lend_factor().start()
        load(last).wait()

    def table_block(j):
        f = j * bins + offset_bin + lax.broadcasted_iota(jnp.int32, (bins, LANES), 0)
        lane = lax.broadcasted_iota(jnp.int32, (bins, LANES), 1)
        unit = 2.0 * math.pi / NT
        fine = lax.rem(f * lane, NT).astype(jnp.float32) * unit
        coarse = lax.rem(f * (lane * LANES), NT).astype(jnp.float32) * unit
        cos_fine, sin_fine = jnp.cos(fine), jnp.sin(fine)
        cos_coarse, sin_coarse = jnp.cos(coarse), jnp.sin(coarse)
        row = pl.multiple_of(j * (2 * bins), 2 * bins)
        for a in range(NT // LANES):
            ca = cos_coarse[:, a:a + 1]
            sa = sin_coarse[:, a:a + 1]
            at = slice(a * LANES, (a + 1) * LANES)
            table[pl.ds(row, bins), at] = (ca * cos_fine - sa * sin_fine).astype(jnp.bfloat16)
            table[pl.ds(row + bins, bins), at] = (
                -(sa * cos_fine + ca * sin_fine)
            ).astype(jnp.bfloat16)

    width = min(256, modes)

    def couple(source, turn, g, k, shard):
        @pl.loop(0, modes // width)
        def _(tile):
            rows = pl.ds(pl.multiple_of(tile * width, width), width)
            by_real = jnp.zeros((2 * half, width), jnp.float32)
            by_imag = jnp.zeros((2 * half, width), jnp.float32)
            for z in range(n):
                a = amp[g, k, z]
                cols = slice(z * modes, (z + 1) * modes)
                dims = (((1,), (1,)), ((), ()))
                by_real += lax.dot_general(
                    a, source[0, rows, cols], dims, preferred_element_type=jnp.float32
                )
                by_imag += lax.dot_general(
                    a, source[1, rows, cols], dims, preferred_element_type=jnp.float32
                )
            real = (by_real[:half] - by_imag[half:]).reshape(cs, bins, width)
            imag = (by_real[half:] + by_imag[:half]).reshape(cs, bins, width)
            fr = turn[0, :, rows][None]
            fi = turn[1, :, rows][None]
            amp[g + 1, k, shard, 0:half, rows] = (
                (real * fr - imag * fi).reshape(half, width).astype(jnp.bfloat16)
            )
            amp[g + 1, k, shard, half:2 * half, rows] = (
                (real * fi + imag * fr).reshape(half, width).astype(jnp.bfloat16)
            )

    @pl.loop(0, phases)
    def _(p):
        g, position = phase(p)
        k = owner(position)
        active = wanted(g, me)
        helping = jnp.logical_and(g == last, helper)

        @pl.when(jnp.logical_and(g == 0, position + 2 < n))
        def _():
            send_own(0, owner(position + 2))

        if relieve:
            @pl.when(jnp.logical_and(edge, p < lending))
            def _():
                @pl.loop(p * pieces // lending, (p + 1) * pieces // lending)
                def _(q):
                    lend(q).start()

        for d in range(n - 1):
            for sign in (lead, -lead):
                @pl.when(jnp.logical_and(active, inside(me - sign * (d + 1))))
                def _(sign=sign, d=d):
                    arrival(g, k, sign, d).wait_recv()
                    if d + 1 < n - 1:
                        @pl.when(wanted(g, me + sign))
                        def _():
                            hop(g, k, sign, d + 1).start()

        @pl.when(jnp.logical_and(position == 0, active))
        def _():
            load(g).wait()

        @pl.when(active)
        def _():
            couple(matrix.at[g], factor.at[g], g, k, me)

        @pl.when(g < last)
        def _():
            send_own(g + 1, k)

        @pl.when(jnp.logical_and(jnp.logical_and(g == last, active), k != me))
        def _():
            to_owner(k, me, 0).start()

        if relieve:
            @pl.when(helping)
            def _():
                @pl.when(position == 0)
                def _():
                    lend_factor().wait_recv()

                    @pl.loop(0, pieces)
                    def _(q):
                        lend(q).wait_recv()

                couple(lent, lent_factor, last, k, partner)

                @pl.when(k != me)
                def _():
                    to_owner(k, partner, 1).start()

        @pl.loop(0, (nf - p + phases - 1) // phases)
        def _(i):
            table_block(p + i * phases)

    @pl.loop(0, n)
    def _(z):
        here = jnp.logical_or(
            jnp.logical_and(z == me, jnp.logical_not(edge)),
            jnp.logical_and(helper, z == partner),
        )

        @pl.when(jnp.logical_not(here))
        def _():
            sender = jnp.where(at_end(z), jnp.where(z == 0, 1, n - 2), z)
            pltpu.make_async_remote_copy(
                src_ref=amp.at[segments, me, z],
                dst_ref=amp.at[segments, me, z],
                send_sem=own_send.at[me, 0],
                recv_sem=own_recv.at[z],
                device_id={"mode": sender},
                device_id_type=pl.DeviceIdType.MESH,
            ).wait_recv()

    field = jnp.zeros((2 * half, receivers), jnp.float32)
    for z in range(n):
        field += jnp.dot(
            amp[segments, me, z], shapes[0, z * modes:(z + 1) * modes, :],
            preferred_element_type=jnp.float32,
        )
    wr, wi = weights[:, 0:1], weights[:, 1:2]
    fr, fi = field[:half], field[half:]
    weighted[0] = (wr * fr - wi * fi).T.astype(jnp.bfloat16)
    weighted[1] = (wr * fi + wi * fr).T.astype(jnp.bfloat16)

    def to_receiver(j, slot):
        return pltpu.make_async_remote_copy(
            src_ref=weighted.at[:, pl.ds(pl.multiple_of(j * rh, rh), rh)],
            dst_ref=landed.at[slot],
            send_sem=out_send.at[j],
            recv_sem=out_recv.at[slot],
            device_id={"freq": j},
            device_id_type=pl.DeviceIdType.MESH,
        )

    @pl.loop(1, nf)
    def _(i):
        to_receiver(lax.rem(band + i, nf), band).start()

    received[band] = weighted[:, pl.ds(pl.multiple_of(band * rh, rh), rh), :]

    @pl.loop(1, nf)
    def _(i):
        j = lax.rem(band + i, nf)
        to_receiver(j, j).wait_recv()
        received[j] = landed[j]

    @pl.loop(1, nf)
    def _(i):
        to_receiver(lax.rem(band + i, nf), band).wait_send()

    @pl.loop(0, phases)
    def _(p):
        g = p // n
        k = lax.rem(p, n)
        for d in range(n - 1):
            for sign in (lead, -lead):
                @pl.when(jnp.logical_and(inside(me - sign * d), wanted(g, me + sign)))
                def _(sign=sign, d=d):
                    hop(g, k, sign, d).wait_send()

    @pl.loop(1, n)
    def _(i):
        k = lax.rem(me + i, n)

        @pl.when(jnp.logical_not(edge))
        def _():
            to_owner(k, me, 0).wait_send()

        if relieve:
            @pl.when(helper)
            def _():
                to_owner(k, partner, 1).wait_send()

    if relieve:
        @pl.when(edge)
        def _():
            lend_factor().wait_send()

            @pl.loop(0, pieces)
            def _(q):
                lend(q).wait_send()


def shards(excitation, coupling, wavenumber, mode_counts, seg_steps, shapes, spectrum):
    n = lax.axis_size("mode")
    nf = lax.axis_size("freq")
    sources, _, bins, modes = excitation.shape
    segments, _, _, _, all_modes = coupling.shape
    receivers = shapes.shape[-1]
    cs = sources // n
    half = cs * bins
    rh = receivers // nf
    all_bins = bins * nf
    vmem = pl.BlockSpec(memory_space=pltpu.VMEM)
    dma = pltpu.SemaphoreType.DMA
    table, received = pl.pallas_call(
        functools.partial(propagate, n, nf, all_bins // 16),
        out_shape=(
            jax.ShapeDtypeStruct((nf * 2 * bins, NT), jnp.bfloat16),
            jax.ShapeDtypeStruct((nf, 2, rh, half), jnp.bfloat16),
        ),
        in_specs=[
            vmem, pl.BlockSpec(memory_space=pl.ANY), vmem, vmem,
            pl.BlockSpec(memory_space=pltpu.SMEM), vmem, vmem,
        ],
        out_specs=(vmem, vmem),
        scratch_shapes=[
            pltpu.VMEM((segments, 2, modes, all_modes), jnp.bfloat16),
            pltpu.VMEM((segments + 1, n, n, 2 * half, modes), jnp.bfloat16),
            pltpu.VMEM((segments, 2, bins, modes), jnp.float32),
            pltpu.VMEM((2, receivers, half), jnp.bfloat16),
            pltpu.VMEM((nf, 2, rh, half), jnp.bfloat16),
            pltpu.VMEM((2, modes, all_modes), jnp.bfloat16),
            pltpu.VMEM((2, bins, modes), jnp.float32),
            dma((segments,)),
            dma((segments, n, 2, n - 1)),
            dma((segments, n, 2, n - 1)),
            dma((n, 2)),
            dma((n,)),
            dma((nf,)),
            dma((nf,)),
            dma((max(segments - 1, 1) * n,)),
            dma((max(segments - 1, 1) * n,)),
            dma((2,)),
        ],
        compiler_params=pltpu.CompilerParams(
            collective_id=0, has_side_effects=True, vmem_limit_bytes=60 * 1024 * 1024
        ),
        name="propagate",
    )(
        excitation, coupling, wavenumber, mode_counts.reshape(bins, 1), seg_steps, shapes,
        jnp.tile(spectrum.T, (cs, 1)),
    )
    left = received.reshape(nf, 2, rh, cs, bins).transpose(3, 2, 0, 1, 4)
    left = left.reshape(cs, rh, nf * 2 * bins)
    summed = lax.dot_general(
        left, table, (((2,), (0,)), ((), ())), preferred_element_type=jnp.float32
    )
    return summed * (1.0 / math.sqrt(all_bins))


def solution(mesh):
    in_specs = (
        P(None, None, "freq", "mode"),
        P(None, "freq", None, "mode", None),
        P("freq", "mode"),
        P("freq"),
        P(),
        P("freq", None, None),
        P(None, "freq"),
    )
    out_specs = P("mode", "freq", None)
    return jax.shard_map(shards, mesh=mesh, in_specs=in_specs, out_specs=out_specs, check_vma=False)
```

```python
import functools
import math

import jax
import jax.numpy as jnp
from jax import lax
from jax.experimental import pallas as pl
from jax.experimental.pallas import tpu as pltpu
from jax.sharding import PartitionSpec as P

NT = 4096
LANES = 128


def phase_order(segments, n):
    pairs = [(g, position) for g in range(segments) for position in range(n)]
    return sorted(pairs, key=lambda pair: (pair[1] + pair[0] * 0.625 * n, pair[0]))


def propagate(
    n, nf, offset_bin, exc, coupling, wavenumber, counts, steps, shapes, weights,
    table, received,
    matrix, amp, factor, weighted, landed, lent, lent_factor,
    load_sem, send_sem, recv_sem, own_send, own_recv, out_send, out_recv,
    lend_send, lend_recv, lend_factor_sem,
):
    segments = coupling.shape[0]
    sources, _, bins, modes = exc.shape
    cs = sources // n
    half = cs * bins
    receivers = shapes.shape[-1]
    rh = receivers // nf
    phases = segments * n
    me = lax.axis_index("mode")
    band = lax.axis_index("freq")

    relieve = n >= 4 and segments >= 2
    last = segments - 1
    order = phase_order(segments, n)
    first_last = [g for g, _ in order].index(last)
    lending = max(first_last - 1, 1)
    pieces = max(last, 1) * n
    piece = modes // pieces

    def at_end(z):
        return jnp.logical_and(relieve, jnp.logical_or(z == 0, z == n - 1))

    edge = at_end(me)
    helper = jnp.logical_and(relieve, jnp.logical_or(me == 1, me == n - 2))
    partner = jnp.where(me == 1, 0, n - 1)
    inward = jnp.where(me == 0, min(1, n - 1), max(n - 2, 0))

    def owner(position):
        return jnp.where(
            lax.rem(position, 2) == 0, position // 2, n - 1 - position // 2
        )

    def phase(p):
        g, position = jnp.int32(0), jnp.int32(0)
        for i, (at_g, at_position) in enumerate(order):
            g = jnp.where(p == i, at_g, g)
            position = jnp.where(p == i, at_position, position)
        return g, position

    def lend(q):
        rows = pl.ds(pl.multiple_of(q * piece, piece), piece)
        return pltpu.make_async_remote_copy(
            src_ref=matrix.at[last, :, rows],
            dst_ref=lent.at[:, rows],
            send_sem=lend_send.at[q],
            recv_sem=lend_recv.at[q],
            device_id={"mode": inward},
            device_id_type=pl.DeviceIdType.MESH,
        )

    def lend_factor():
        return pltpu.make_async_remote_copy(
            src_ref=factor.at[last],
            dst_ref=lent_factor,
            send_sem=lend_factor_sem.at[0],
            recv_sem=lend_factor_sem.at[1],
            device_id={"mode": inward},
            device_id_type=pl.DeviceIdType.MESH,
        )

    def load(g):
        return pltpu.make_async_copy(coupling.at[g, 0], matrix.at[g], load_sem.at[g])

    def hop(g, k, sign, d):
        shard = me - sign * d
        way = (sign + 1) // 2
        return pltpu.make_async_remote_copy(
            src_ref=amp.at[g, k, shard],
            dst_ref=amp.at[g, k, shard],
            send_sem=send_sem.at[g, k, way, d],
            recv_sem=recv_sem.at[g, k, way, d],
            device_id={"mode": me + sign},
            device_id_type=pl.DeviceIdType.MESH,
        )

    def arrival(g, k, sign, d):
        shard = me - sign * (d + 1)
        way = (sign + 1) // 2
        return pltpu.make_async_remote_copy(
            src_ref=amp.at[g, k, shard],
            dst_ref=amp.at[g, k, shard],
            send_sem=send_sem.at[g, k, way, d],
            recv_sem=recv_sem.at[g, k, way, d],
            device_id={"mode": me - sign},
            device_id_type=pl.DeviceIdType.MESH,
        )

    def inside(z):
        return jnp.logical_and(z >= 0, z < n)

    lead = jnp.where(me < n // 2, -1, 1)

    def wanted(g, z):
        return jnp.logical_and(inside(z), jnp.logical_not(jnp.logical_and(g == last, at_end(z))))

    def send_own(g, k):
        for sign in (lead, -lead):
            @pl.when(wanted(g, me + sign))
            def _(sign=sign):
                hop(g, k, sign, 0).start()

    def to_owner(k, shard, which):
        return pltpu.make_async_remote_copy(
            src_ref=amp.at[segments, k, shard],
            dst_ref=amp.at[segments, k, shard],
            send_sem=own_send.at[k, which],
            recv_sem=own_recv.at[shard],
            device_id={"mode": k},
            device_id_type=pl.DeviceIdType.MESH,
        )

    for g in range(segments):
        load(g).start()

    barrier = pltpu.get_barrier_semaphore()

    @pl.loop(1, n)
    def _(i):
        pl.semaphore_signal(
            barrier, inc=1, device_id={"mode": lax.rem(me + i, n)},
            device_id_type=pl.DeviceIdType.MESH,
        )

    @pl.loop(1, nf)
    def _(i):
        pl.semaphore_signal(
            barrier, inc=1, device_id={"freq": lax.rem(band + i, nf)},
            device_id_type=pl.DeviceIdType.MESH,
        )

    mode_number = me * modes + lax.broadcasted_iota(jnp.int32, (bins, modes), 1)
    living = jnp.where(mode_number < counts[...], 1.0, 0.0).astype(jnp.float32)

    @pl.loop(0, n)
    def _(k):
        for c in range(2):
            x = exc[pl.ds(k * cs, cs), c].astype(jnp.float32) * living[None]
            amp[0, k, me, c * half:(c + 1) * half, :] = (
                x.reshape(half, modes).astype(jnp.bfloat16)
            )

    pl.semaphore_wait(barrier, n - 1 + nf - 1)
    send_own(0, owner(jnp.int32(0)))
    if n > 1:
        send_own(0, owner(jnp.int32(1)))

    for g in range(segments):
        angle = wavenumber[...] * steps[g].astype(jnp.float32)
        factor[g, 0] = living * jnp.cos(angle)
        factor[g, 1] = living * jnp.sin(angle)

    @pl.when(edge)
    def _():
        lend_factor().start()
        load(last).wait()

    def table_block(j):
        f = j * bins + offset_bin + lax.broadcasted_iota(jnp.int32, (bins, LANES), 0)
        lane = lax.broadcasted_iota(jnp.int32, (bins, LANES), 1)
        unit = 2.0 * math.pi / NT
        fine = lax.rem(f * lane, NT).astype(jnp.float32) * unit
        coarse = lax.rem(f * (lane * LANES), NT).astype(jnp.float32) * unit
        cos_fine, sin_fine = jnp.cos(fine), jnp.sin(fine)
        cos_coarse, sin_coarse = jnp.cos(coarse), jnp.sin(coarse)
        row = pl.multiple_of(j * (2 * bins), 2 * bins)
        for a in range(NT // LANES):
            ca = cos_coarse[:, a:a + 1]
            sa = sin_coarse[:, a:a + 1]
            at = slice(a * LANES, (a + 1) * LANES)
            table[pl.ds(row, bins), at] = (ca * cos_fine - sa * sin_fine).astype(jnp.bfloat16)
            table[pl.ds(row + bins, bins), at] = (
                -(sa * cos_fine + ca * sin_fine)
            ).astype(jnp.bfloat16)

    width = min(256, modes)

    def forward(p, d):
        g, position = phase(p)
        k = owner(position)
        for sign in (lead, -lead):
            @pl.when(
                jnp.logical_and(
                    jnp.logical_and(p < phases, wanted(g, me)),
                    jnp.logical_and(inside(me - sign * (d + 1)), wanted(g, me + sign)),
                )
            )
            def _(sign=sign):
                arrival(g, k, sign, d).wait_recv()
                hop(g, k, sign, d + 1).start()

    tiles = modes // width

    def couple(source, turn, g, k, shard, tile):
        rows = slice(tile * width, (tile + 1) * width)
        by_real = jnp.zeros((2 * half, width), jnp.float32)
        by_imag = jnp.zeros((2 * half, width), jnp.float32)
        for z in range(n):
            a = amp[g, k, z]
            cols = slice(z * modes, (z + 1) * modes)
            dims = (((1,), (1,)), ((), ()))
            by_real += lax.dot_general(
                a, source[0, rows, cols], dims, preferred_element_type=jnp.float32
            )
            by_imag += lax.dot_general(
                a, source[1, rows, cols], dims, preferred_element_type=jnp.float32
            )
        real = (by_real[:half] - by_imag[half:]).reshape(cs, bins, width)
        imag = (by_real[half:] + by_imag[:half]).reshape(cs, bins, width)
        fr = turn[0, :, rows][None]
        fi = turn[1, :, rows][None]
        amp[g + 1, k, shard, 0:half, rows] = (
            (real * fr - imag * fi).reshape(half, width).astype(jnp.bfloat16)
        )
        amp[g + 1, k, shard, half:2 * half, rows] = (
            (real * fi + imag * fr).reshape(half, width).astype(jnp.bfloat16)
        )

    for d in range(n - 2):
        forward(jnp.int32(0), d)

    @pl.loop(0, phases)
    def _(p):
        g, position = phase(p)
        k = owner(position)
        active = wanted(g, me)
        helping = jnp.logical_and(g == last, helper)

        @pl.when(jnp.logical_and(g == 0, position + 2 < n))
        def _():
            send_own(0, owner(position + 2))

        if relieve:
            @pl.when(jnp.logical_and(edge, p < lending))
            def _():
                @pl.loop(p * pieces // lending, (p + 1) * pieces // lending)
                def _(q):
                    lend(q).start()

        if n > 2:
            forward(p + 1, 0)

        for d in range(n - 1):
            for sign in (lead, -lead):
                @pl.when(
                    jnp.logical_and(
                        jnp.logical_and(active, inside(me - sign * (d + 1))),
                        jnp.logical_not(wanted(g, me + sign)),
                    )
                )
                def _(sign=sign, d=d):
                    arrival(g, k, sign, d).wait_recv()

        @pl.when(jnp.logical_and(position == 0, active))
        def _():
            load(g).wait()

        for tile in range(tiles):
            @pl.when(active)
            def _(tile=tile):
                couple(matrix.at[g], factor.at[g], g, k, me, tile)

            if tile + 1 < n - 2:
                forward(p + 1, tile + 1)
        for d in range(tiles + 1, n - 2):
            forward(p + 1, d)

        @pl.when(g < last)
        def _():
            send_own(g + 1, k)

        @pl.when(jnp.logical_and(jnp.logical_and(g == last, active), k != me))
        def _():
            to_owner(k, me, 0).start()

        if relieve:
            @pl.when(helping)
            def _():
                @pl.when(position == 0)
                def _():
                    lend_factor().wait_recv()

                    @pl.loop(0, pieces)
                    def _(q):
                        lend(q).wait_recv()

                for tile in range(tiles):
                    couple(lent, lent_factor, last, k, partner, tile)

                @pl.when(k != me)
                def _():
                    to_owner(k, partner, 1).start()

        @pl.loop(0, (nf - p + phases - 1) // phases)
        def _(i):
            table_block(p + i * phases)

    @pl.loop(0, n)
    def _(z):
        here = jnp.logical_or(
            jnp.logical_and(z == me, jnp.logical_not(edge)),
            jnp.logical_and(helper, z == partner),
        )

        @pl.when(jnp.logical_not(here))
        def _():
            sender = jnp.where(at_end(z), jnp.where(z == 0, 1, n - 2), z)
            pltpu.make_async_remote_copy(
                src_ref=amp.at[segments, me, z],
                dst_ref=amp.at[segments, me, z],
                send_sem=own_send.at[me, 0],
                recv_sem=own_recv.at[z],
                device_id={"mode": sender},
                device_id_type=pl.DeviceIdType.MESH,
            ).wait_recv()

    field = jnp.zeros((2 * half, receivers), jnp.float32)
    for z in range(n):
        field += jnp.dot(
            amp[segments, me, z], shapes[0, z * modes:(z + 1) * modes, :],
            preferred_element_type=jnp.float32,
        )
    wr, wi = weights[:, 0:1], weights[:, 1:2]
    fr, fi = field[:half], field[half:]
    weighted[0] = (wr * fr - wi * fi).T.astype(jnp.bfloat16)
    weighted[1] = (wr * fi + wi * fr).T.astype(jnp.bfloat16)

    def to_receiver(j, slot):
        return pltpu.make_async_remote_copy(
            src_ref=weighted.at[:, pl.ds(pl.multiple_of(j * rh, rh), rh)],
            dst_ref=landed.at[slot],
            send_sem=out_send.at[j],
            recv_sem=out_recv.at[slot],
            device_id={"freq": j},
            device_id_type=pl.DeviceIdType.MESH,
        )

    @pl.loop(1, nf)
    def _(i):
        to_receiver(lax.rem(band + i, nf), band).start()

    received[band] = weighted[:, pl.ds(pl.multiple_of(band * rh, rh), rh), :]

    @pl.loop(1, nf)
    def _(i):
        j = lax.rem(band + i, nf)
        to_receiver(j, j).wait_recv()
        received[j] = landed[j]

    @pl.loop(1, nf)
    def _(i):
        to_receiver(lax.rem(band + i, nf), band).wait_send()

    @pl.loop(0, phases)
    def _(p):
        g = p // n
        k = lax.rem(p, n)
        for d in range(n - 1):
            for sign in (lead, -lead):
                @pl.when(jnp.logical_and(inside(me - sign * d), wanted(g, me + sign)))
                def _(sign=sign, d=d):
                    hop(g, k, sign, d).wait_send()

    @pl.loop(1, n)
    def _(i):
        k = lax.rem(me + i, n)

        @pl.when(jnp.logical_not(edge))
        def _():
            to_owner(k, me, 0).wait_send()

        if relieve:
            @pl.when(helper)
            def _():
                to_owner(k, partner, 1).wait_send()

    if relieve:
        @pl.when(edge)
        def _():
            lend_factor().wait_send()

            @pl.loop(0, pieces)
            def _(q):
                lend(q).wait_send()


def shards(excitation, coupling, wavenumber, mode_counts, seg_steps, shapes, spectrum):
    n = lax.axis_size("mode")
    nf = lax.axis_size("freq")
    sources, _, bins, modes = excitation.shape
    segments, _, _, _, all_modes = coupling.shape
    receivers = shapes.shape[-1]
    cs = sources // n
    half = cs * bins
    rh = receivers // nf
    all_bins = bins * nf
    vmem = pl.BlockSpec(memory_space=pltpu.VMEM)
    dma = pltpu.SemaphoreType.DMA
    table, received = pl.pallas_call(
        functools.partial(propagate, n, nf, all_bins // 16),
        out_shape=(
            jax.ShapeDtypeStruct((nf * 2 * bins, NT), jnp.bfloat16),
            jax.ShapeDtypeStruct((nf, 2, rh, half), jnp.bfloat16),
        ),
        in_specs=[
            vmem, pl.BlockSpec(memory_space=pl.ANY), vmem, vmem,
            pl.BlockSpec(memory_space=pltpu.SMEM), vmem, vmem,
        ],
        out_specs=(vmem, vmem),
        scratch_shapes=[
            pltpu.VMEM((segments, 2, modes, all_modes), jnp.bfloat16),
            pltpu.VMEM((segments + 1, n, n, 2 * half, modes), jnp.bfloat16),
            pltpu.VMEM((segments, 2, bins, modes), jnp.float32),
            pltpu.VMEM((2, receivers, half), jnp.bfloat16),
            pltpu.VMEM((nf, 2, rh, half), jnp.bfloat16),
            pltpu.VMEM((2, modes, all_modes), jnp.bfloat16),
            pltpu.VMEM((2, bins, modes), jnp.float32),
            dma((segments,)),
            dma((segments, n, 2, n - 1)),
            dma((segments, n, 2, n - 1)),
            dma((n, 2)),
            dma((n,)),
            dma((nf,)),
            dma((nf,)),
            dma((max(segments - 1, 1) * n,)),
            dma((max(segments - 1, 1) * n,)),
            dma((2,)),
        ],
        compiler_params=pltpu.CompilerParams(
            collective_id=0, has_side_effects=True, vmem_limit_bytes=60 * 1024 * 1024
        ),
        name="propagate",
    )(
        excitation, coupling, wavenumber, mode_counts.reshape(bins, 1), seg_steps, shapes,
        jnp.tile(spectrum.T, (cs, 1)),
    )
    left = received.reshape(nf, 2, rh, cs, bins).transpose(3, 2, 0, 1, 4)
    left = left.reshape(cs, rh, nf * 2 * bins)
    summed = lax.dot_general(
        left, table, (((2,), (0,)), ((), ())), preferred_element_type=jnp.float32
    )
    return summed * (1.0 / math.sqrt(all_bins))


def solution(mesh):
    in_specs = (
        P(None, None, "freq", "mode"),
        P(None, "freq", None, "mode", None),
        P("freq", "mode"),
        P("freq"),
        P(),
        P("freq", None, None),
        P(None, "freq"),
    )
    out_specs = P("mode", "freq", None)
    return jax.shard_map(shards, mesh=mesh, in_specs=in_specs, out_specs=out_specs, check_vma=False)
```

```python
import functools
import math

import jax
import jax.numpy as jnp
from jax import lax
from jax.experimental import pallas as pl
from jax.experimental.pallas import tpu as pltpu
from jax.sharding import PartitionSpec as P

NT = 4096
LANES = 128


def phase_order(segments, n):
    def key(pair):
        g, position = pair
        if segments == 3:
            return ((0.0, 0.55, 0.9)[g] * n + (1.0, 0.6, 0.25)[g] * position, g)
        return (position + g * 0.625 * n, g)

    return sorted([(g, position) for g in range(segments) for position in range(n)], key=key)


def propagate(
    n, nf, offset_bin, exc, coupling, wavenumber, counts, steps, shapes, spectrum,
    table, received,
    matrix, amp, factor, weighted, landed, lent, lent_factor, part, mine, total,
    load_sem, send_sem, recv_sem, own_send, own_recv, out_send, out_recv,
    lend_send, lend_recv, lend_factor_sem,
):
    segments = coupling.shape[0]
    sources, _, bins, modes = exc.shape
    cs = sources // n
    half = cs * bins
    receivers = shapes.shape[-1]
    rh = receivers // nf
    phases = segments * n
    me = lax.axis_index("mode")
    band = lax.axis_index("freq")

    relieve = n >= 4 and segments >= 2
    last = segments - 1
    order = phase_order(segments, n)
    first_last = [g for g, _ in order].index(last)
    lending = max(first_last - 1, 1)
    pieces = max(last, 1) * n
    piece = modes // pieces

    def at_end(z):
        return jnp.logical_and(relieve, jnp.logical_or(z == 0, z == n - 1))

    edge = at_end(me)
    helper = jnp.logical_and(relieve, jnp.logical_or(me == 1, me == n - 2))
    partner = jnp.where(me == 1, 0, n - 1)
    inward = jnp.where(me == 0, min(1, n - 1), max(n - 2, 0))

    def owner(position):
        return jnp.where(
            lax.rem(position, 2) == 0, position // 2, n - 1 - position // 2
        )

    def phase(p):
        g, position = jnp.int32(0), jnp.int32(0)
        for i, (at_g, at_position) in enumerate(order):
            g = jnp.where(p == i, at_g, g)
            position = jnp.where(p == i, at_position, position)
        return g, position

    def lend(q):
        rows = pl.ds(pl.multiple_of(q * piece, piece), piece)
        return pltpu.make_async_remote_copy(
            src_ref=matrix.at[last, :, rows],
            dst_ref=lent.at[:, rows],
            send_sem=lend_send.at[q],
            recv_sem=lend_recv.at[q],
            device_id={"mode": inward},
            device_id_type=pl.DeviceIdType.MESH,
        )

    def lend_factor():
        return pltpu.make_async_remote_copy(
            src_ref=factor.at[last],
            dst_ref=lent_factor,
            send_sem=lend_factor_sem.at[0],
            recv_sem=lend_factor_sem.at[1],
            device_id={"mode": inward},
            device_id_type=pl.DeviceIdType.MESH,
        )

    def load(g):
        return pltpu.make_async_copy(coupling.at[g, 0], matrix.at[g], load_sem.at[g])

    def hop(g, k, sign, d):
        shard = me - sign * d
        way = (sign + 1) // 2
        return pltpu.make_async_remote_copy(
            src_ref=amp.at[g, k, shard],
            dst_ref=amp.at[g, k, shard],
            send_sem=send_sem.at[g, k, way, d],
            recv_sem=recv_sem.at[g, k, way, d],
            device_id={"mode": me + sign},
            device_id_type=pl.DeviceIdType.MESH,
        )

    def arrival(g, k, sign, d):
        shard = me - sign * (d + 1)
        way = (sign + 1) // 2
        return pltpu.make_async_remote_copy(
            src_ref=amp.at[g, k, shard],
            dst_ref=amp.at[g, k, shard],
            send_sem=send_sem.at[g, k, way, d],
            recv_sem=recv_sem.at[g, k, way, d],
            device_id={"mode": me - sign},
            device_id_type=pl.DeviceIdType.MESH,
        )

    def inside(z):
        return jnp.logical_and(z >= 0, z < n)

    lead = jnp.where(me < n // 2, -1, 1)

    def wanted(g, z):
        return jnp.logical_and(inside(z), jnp.logical_not(jnp.logical_and(g == last, at_end(z))))

    def send_own(g, k):
        for sign in (lead, -lead):
            @pl.when(wanted(g, me + sign))
            def _(sign=sign):
                hop(g, k, sign, 0).start()

    def to_owner(k):
        return pltpu.make_async_remote_copy(
            src_ref=part.at[0, k],
            dst_ref=part.at[1, me],
            send_sem=own_send.at[k],
            recv_sem=own_recv.at[me],
            device_id={"mode": k},
            device_id_type=pl.DeviceIdType.MESH,
        )

    for g in range(segments):
        load(g).start()

    barrier = pltpu.get_barrier_semaphore()

    @pl.loop(1, n)
    def _(i):
        pl.semaphore_signal(
            barrier, inc=1, device_id={"mode": lax.rem(me + i, n)},
            device_id_type=pl.DeviceIdType.MESH,
        )

    @pl.loop(1, nf)
    def _(i):
        pl.semaphore_signal(
            barrier, inc=1, device_id={"freq": lax.rem(band + i, nf)},
            device_id_type=pl.DeviceIdType.MESH,
        )

    mode_number = me * modes + lax.broadcasted_iota(jnp.int32, (bins, modes), 1)
    row_number = lax.broadcasted_iota(jnp.int32, (bins, modes), 0)
    count = jnp.zeros((bins, modes), jnp.int32)
    for f in range(bins):
        count = jnp.where(row_number == f, counts[f], count)
    living = jnp.where(mode_number < count, 1.0, 0.0).astype(jnp.float32)

    @pl.loop(0, n)
    def _(k):
        for c in range(2):
            x = exc[pl.ds(k * cs, cs), c].astype(jnp.float32) * living[None]
            amp[0, k, me, c * half:(c + 1) * half, :] = (
                x.reshape(half, modes).astype(jnp.bfloat16)
            )

    pl.semaphore_wait(barrier, n - 1 + nf - 1)
    send_own(0, owner(jnp.int32(0)))
    if n > 1:
        send_own(0, owner(jnp.int32(1)))

    def turn_by(g):
        angle = wavenumber[...] * steps[g].astype(jnp.float32)
        factor[g, 0] = living * jnp.cos(angle)
        factor[g, 1] = living * jnp.sin(angle)

    def table_block(j):
        f = j * bins + offset_bin + lax.broadcasted_iota(jnp.int32, (bins, LANES), 0)
        lane = lax.broadcasted_iota(jnp.int32, (bins, LANES), 1)
        unit = 2.0 * math.pi / NT
        fine = lax.rem(f * lane, NT).astype(jnp.float32) * unit
        coarse = lax.rem(f * (lane * LANES), NT).astype(jnp.float32) * unit
        cos_fine, sin_fine = jnp.cos(fine), jnp.sin(fine)
        cos_coarse, sin_coarse = jnp.cos(coarse), jnp.sin(coarse)
        row = pl.multiple_of(j * (2 * bins), 2 * bins)
        for a in range(NT // LANES):
            ca = cos_coarse[:, a:a + 1]
            sa = sin_coarse[:, a:a + 1]
            at = slice(a * LANES, (a + 1) * LANES)
            table[pl.ds(row, bins), at] = (ca * cos_fine - sa * sin_fine).astype(jnp.bfloat16)
            table[pl.ds(row + bins, bins), at] = (
                -(sa * cos_fine + ca * sin_fine)
            ).astype(jnp.bfloat16)

    width = min(256, modes)

    def forward(p, d):
        g, position = phase(p)
        k = owner(position)
        for sign in (lead, -lead):
            @pl.when(
                jnp.logical_and(
                    jnp.logical_and(p < phases, wanted(g, me)),
                    jnp.logical_and(inside(me - sign * (d + 1)), wanted(g, me + sign)),
                )
            )
            def _(sign=sign):
                arrival(g, k, sign, d).wait_recv()
                hop(g, k, sign, d + 1).start()

    tiles = modes // width

    def couple(source, turn, g, k, shard, tile):
        rows = slice(tile * width, (tile + 1) * width)
        by_real = jnp.zeros((2 * half, width), jnp.float32)
        by_imag = jnp.zeros((2 * half, width), jnp.float32)
        for z in range(n):
            a = amp[g, k, z]
            cols = slice(z * modes, (z + 1) * modes)
            dims = (((1,), (1,)), ((), ()))
            by_real += lax.dot_general(
                a, source[0, rows, cols], dims, preferred_element_type=jnp.float32
            )
            by_imag += lax.dot_general(
                a, source[1, rows, cols], dims, preferred_element_type=jnp.float32
            )
        real = (by_real[:half] - by_imag[half:]).reshape(cs, bins, width)
        imag = (by_real[half:] + by_imag[:half]).reshape(cs, bins, width)
        fr = turn[0, :, rows][None]
        fi = turn[1, :, rows][None]
        amp[g + 1, k, shard, 0:half, rows] = (
            (real * fr - imag * fi).reshape(half, width).astype(jnp.bfloat16)
        )
        amp[g + 1, k, shard, half:2 * half, rows] = (
            (real * fi + imag * fr).reshape(half, width).astype(jnp.bfloat16)
        )

    turn_by(0)
    if n > 2:
        forward(jnp.int32(0), 0)
    for g in range(1, segments):
        turn_by(g)

    @pl.when(edge)
    def _():
        lend_factor().start()
        load(last).wait()

    for d in range(1, n - 2):
        forward(jnp.int32(0), d)

    @pl.loop(0, phases)
    def _(p):
        g, position = phase(p)
        k = owner(position)
        active = wanted(g, me)
        helping = jnp.logical_and(g == last, helper)

        @pl.when(jnp.logical_and(g == 0, position + 2 < n))
        def _():
            send_own(0, owner(position + 2))

        if relieve:
            @pl.when(jnp.logical_and(edge, p < lending))
            def _():
                @pl.loop(p * pieces // lending, (p + 1) * pieces // lending)
                def _(q):
                    lend(q).start()

        if n > 2:
            forward(p + 1, 0)

        for d in range(n - 1):
            for sign in (lead, -lead):
                @pl.when(
                    jnp.logical_and(
                        jnp.logical_and(active, inside(me - sign * (d + 1))),
                        jnp.logical_not(wanted(g, me + sign)),
                    )
                )
                def _(sign=sign, d=d):
                    arrival(g, k, sign, d).wait_recv()

        @pl.when(jnp.logical_and(position == 0, active))
        def _():
            load(g).wait()

        for tile in range(tiles):
            @pl.when(active)
            def _(tile=tile):
                couple(matrix.at[g], factor.at[g], g, k, me, tile)

            if tile + 1 < n - 2:
                forward(p + 1, tile + 1)
        for d in range(tiles + 1, n - 2):
            forward(p + 1, d)

        @pl.when(g < last)
        def _():
            send_own(g + 1, k)

        if relieve:
            @pl.when(helping)
            def _():
                @pl.when(position == 0)
                def _():
                    lend_factor().wait_recv()

                    @pl.loop(0, pieces)
                    def _(q):
                        lend(q).wait_recv()

                for tile in range(tiles):
                    couple(lent, lent_factor, last, k, partner, tile)

        def field_of(shard):
            rows = pl.ds(pl.multiple_of(shard * modes, modes), modes)
            return jnp.dot(
                amp[segments, k, shard], shapes[0, rows, :],
                preferred_element_type=jnp.float32,
            )

        @pl.when(jnp.logical_and(g == last, active))
        def _():
            mine[...] = field_of(me)

            if relieve:
                @pl.when(helper)
                def _():
                    mine[...] += field_of(partner)

            @pl.when(k != me)
            def _():
                part[0, k] = mine[...].astype(jnp.bfloat16)
                to_owner(k).start()

            @pl.when(k == me)
            def _():
                total[...] = mine[...]

        @pl.loop(0, (nf - p + phases - 1) // phases)
        def _(i):
            table_block(p + i * phases)

    @pl.when(edge)
    def _():
        total[...] = jnp.zeros_like(total)

    @pl.loop(1, n)
    def _(i):
        z = lax.rem(me + i, n)

        @pl.when(jnp.logical_not(at_end(z)))
        def _():
            pltpu.make_async_remote_copy(
                src_ref=part.at[0, z],
                dst_ref=part.at[1, z],
                send_sem=own_send.at[z],
                recv_sem=own_recv.at[z],
                device_id={"mode": z},
                device_id_type=pl.DeviceIdType.MESH,
            ).wait_recv()
            total[...] += part[1, z].astype(jnp.float32)

    def weight(c):
        row = lax.broadcasted_iota(jnp.int32, (bins, receivers), 0)
        value = jnp.zeros((bins, receivers), jnp.float32)
        for f in range(bins):
            value = jnp.where(row == f, spectrum[c, f], value)
        return value[None]

    wr, wi = weight(0), weight(1)
    fr = total[0:half].reshape(cs, bins, receivers)
    fi = total[half:2 * half].reshape(cs, bins, receivers)
    weighted[0] = (wr * fr - wi * fi).reshape(half, receivers).T.astype(jnp.bfloat16)
    weighted[1] = (wr * fi + wi * fr).reshape(half, receivers).T.astype(jnp.bfloat16)

    def to_receiver(j, slot):
        return pltpu.make_async_remote_copy(
            src_ref=weighted.at[:, pl.ds(pl.multiple_of(j * rh, rh), rh)],
            dst_ref=landed.at[slot],
            send_sem=out_send.at[j],
            recv_sem=out_recv.at[slot],
            device_id={"freq": j},
            device_id_type=pl.DeviceIdType.MESH,
        )

    @pl.loop(1, nf)
    def _(i):
        to_receiver(lax.rem(band + i, nf), band).start()

    received[band] = weighted[:, pl.ds(pl.multiple_of(band * rh, rh), rh), :]

    @pl.loop(1, nf)
    def _(i):
        j = lax.rem(band + i, nf)
        to_receiver(j, j).wait_recv()
        received[j] = landed[j]

    @pl.loop(1, nf)
    def _(i):
        to_receiver(lax.rem(band + i, nf), band).wait_send()

    @pl.loop(0, phases)
    def _(p):
        g = p // n
        k = lax.rem(p, n)
        for d in range(n - 1):
            for sign in (lead, -lead):
                @pl.when(jnp.logical_and(inside(me - sign * d), wanted(g, me + sign)))
                def _(sign=sign, d=d):
                    hop(g, k, sign, d).wait_send()

    @pl.loop(1, n)
    def _(i):
        k = lax.rem(me + i, n)

        @pl.when(jnp.logical_not(edge))
        def _():
            to_owner(k).wait_send()

    if relieve:
        @pl.when(edge)
        def _():
            lend_factor().wait_send()

            @pl.loop(0, pieces)
            def _(q):
                lend(q).wait_send()


def shards(excitation, coupling, wavenumber, mode_counts, seg_steps, shapes, spectrum):
    n = lax.axis_size("mode")
    nf = lax.axis_size("freq")
    sources, _, bins, modes = excitation.shape
    segments, _, _, _, all_modes = coupling.shape
    receivers = shapes.shape[-1]
    cs = sources // n
    half = cs * bins
    rh = receivers // nf
    all_bins = bins * nf
    vmem = pl.BlockSpec(memory_space=pltpu.VMEM)
    smem = pl.BlockSpec(memory_space=pltpu.SMEM)
    dma = pltpu.SemaphoreType.DMA
    table, received = pl.pallas_call(
        functools.partial(propagate, n, nf, all_bins // 16),
        out_shape=(
            jax.ShapeDtypeStruct((nf * 2 * bins, NT), jnp.bfloat16),
            jax.ShapeDtypeStruct((nf, 2, rh, half), jnp.bfloat16),
        ),
        in_specs=[
            vmem, pl.BlockSpec(memory_space=pl.ANY), vmem, smem, smem, vmem, smem,
        ],
        out_specs=(vmem, vmem),
        scratch_shapes=[
            pltpu.VMEM((segments, 2, modes, all_modes), jnp.bfloat16),
            pltpu.VMEM((segments + 1, n, n, 2 * half, modes), jnp.bfloat16),
            pltpu.VMEM((segments, 2, bins, modes), jnp.float32),
            pltpu.VMEM((2, receivers, half), jnp.bfloat16),
            pltpu.VMEM((nf, 2, rh, half), jnp.bfloat16),
            pltpu.VMEM((2, modes, all_modes), jnp.bfloat16),
            pltpu.VMEM((2, bins, modes), jnp.float32),
            pltpu.VMEM((2, n, 2 * half, receivers), jnp.bfloat16),
            pltpu.VMEM((2 * half, receivers), jnp.float32),
            pltpu.VMEM((2 * half, receivers), jnp.float32),
            dma((segments,)),
            dma((segments, n, 2, n - 1)),
            dma((segments, n, 2, n - 1)),
            dma((n,)),
            dma((n,)),
            dma((nf,)),
            dma((nf,)),
            dma((max(segments - 1, 1) * n,)),
            dma((max(segments - 1, 1) * n,)),
            dma((2,)),
        ],
        compiler_params=pltpu.CompilerParams(
            collective_id=0, has_side_effects=True, vmem_limit_bytes=60 * 1024 * 1024
        ),
        name="propagate",
    )(
        excitation, coupling, wavenumber, mode_counts, seg_steps, shapes, spectrum,
    )
    left = received.reshape(nf, 2, rh, cs, bins).transpose(3, 2, 0, 1, 4)
    left = left.reshape(cs, rh, nf * 2 * bins)
    summed = lax.dot_general(
        left, table, (((2,), (0,)), ((), ())), preferred_element_type=jnp.float32
    )
    return summed * (1.0 / math.sqrt(all_bins))


def solution(mesh):
    in_specs = (
        P(None, None, "freq", "mode"),
        P(None, "freq", None, "mode", None),
        P("freq", "mode"),
        P("freq"),
        P(),
        P("freq", None, None),
        P(None, "freq"),
    )
    out_specs = P("mode", "freq", None)
    return jax.shard_map(shards, mesh=mesh, in_specs=in_specs, out_specs=out_specs, check_vma=False)
```

```python
import functools
import math

import jax
import jax.numpy as jnp
from jax import lax
from jax.experimental import pallas as pl
from jax.experimental.pallas import tpu as pltpu
from jax.sharding import PartitionSpec as P

NT = 4096
LANES = 128


def phase_order(segments, n):
    def key(pair):
        g, position = pair
        if segments == 3:
            return ((0.0, 0.55, 0.9)[g] * n + (1.0, 0.6, 0.25)[g] * position, g)
        return (position + g * 0.625 * n, g)

    return sorted([(g, position) for g in range(segments) for position in range(n)], key=key)


def propagate(
    n, nf, offset_bin, exc, coupling, wavenumber, counts, steps, shapes, spectrum,
    table, received,
    matrix, amp, factor, weighted, landed, lent, lent_narrow, narrow, lent_factor, part, mine, total,
    load_sem, send_sem, recv_sem, own_send, own_recv, out_send, out_recv,
    lend_send, lend_recv, lend_factor_sem,
):
    segments = coupling.shape[0]
    sources, _, bins, modes = exc.shape
    cs = sources // n
    half = cs * bins
    receivers = shapes.shape[-1]
    rh = receivers // nf
    phases = segments * n
    me = lax.axis_index("mode")
    band = lax.axis_index("freq")

    relieve = n >= 4 and segments >= 2
    last = segments - 1
    order = phase_order(segments, n)
    first_last = [g for g, _ in order].index(last)
    lending = max(first_last - 1, 1)
    pieces = max(last, 1) * n
    piece = modes // pieces

    def at_end(z):
        return jnp.logical_and(relieve, jnp.logical_or(z == 0, z == n - 1))

    edge = at_end(me)
    helper = jnp.logical_and(relieve, jnp.logical_or(me == 1, me == n - 2))
    partner = jnp.where(me == 1, 0, n - 1)
    inward = jnp.where(me == 0, min(1, n - 1), max(n - 2, 0))

    def owner(position):
        return jnp.where(
            lax.rem(position, 2) == 0, position // 2, n - 1 - position // 2
        )

    def phase(p):
        g, position = jnp.int32(0), jnp.int32(0)
        for i, (at_g, at_position) in enumerate(order):
            g = jnp.where(p == i, at_g, g)
            position = jnp.where(p == i, at_position, position)
        return g, position

    def lend(q):
        rows = pl.ds(pl.multiple_of(q * piece, piece), piece)
        return pltpu.make_async_remote_copy(
            src_ref=matrix.at[last, :, rows],
            dst_ref=lent.at[:, rows],
            send_sem=lend_send.at[q],
            recv_sem=lend_recv.at[q],
            device_id={"mode": inward},
            device_id_type=pl.DeviceIdType.MESH,
        )

    def lend_factor():
        return pltpu.make_async_remote_copy(
            src_ref=narrow,
            dst_ref=lent_narrow,
            send_sem=lend_factor_sem.at[0],
            recv_sem=lend_factor_sem.at[1],
            device_id={"mode": inward},
            device_id_type=pl.DeviceIdType.MESH,
        )

    def load(g):
        return pltpu.make_async_copy(coupling.at[g, 0], matrix.at[g], load_sem.at[g])

    def hop(g, k, sign, d):
        shard = me - sign * d
        way = (sign + 1) // 2
        return pltpu.make_async_remote_copy(
            src_ref=amp.at[g, k, shard],
            dst_ref=amp.at[g, k, shard],
            send_sem=send_sem.at[g, k, way, d],
            recv_sem=recv_sem.at[g, k, way, d],
            device_id={"mode": me + sign},
            device_id_type=pl.DeviceIdType.MESH,
        )

    def arrival(g, k, sign, d):
        shard = me - sign * (d + 1)
        way = (sign + 1) // 2
        return pltpu.make_async_remote_copy(
            src_ref=amp.at[g, k, shard],
            dst_ref=amp.at[g, k, shard],
            send_sem=send_sem.at[g, k, way, d],
            recv_sem=recv_sem.at[g, k, way, d],
            device_id={"mode": me - sign},
            device_id_type=pl.DeviceIdType.MESH,
        )

    def inside(z):
        return jnp.logical_and(z >= 0, z < n)

    lead = jnp.where(me < n // 2, -1, 1)

    def wanted(g, z):
        return jnp.logical_and(inside(z), jnp.logical_not(jnp.logical_and(g == last, at_end(z))))

    def send_own(g, k):
        for sign in (lead, -lead):
            @pl.when(wanted(g, me + sign))
            def _(sign=sign):
                hop(g, k, sign, 0).start()

    def to_owner(k):
        return pltpu.make_async_remote_copy(
            src_ref=part.at[0, k],
            dst_ref=part.at[1, me],
            send_sem=own_send.at[k],
            recv_sem=own_recv.at[me],
            device_id={"mode": k},
            device_id_type=pl.DeviceIdType.MESH,
        )

    for g in range(segments):
        load(g).start()

    barrier = pltpu.get_barrier_semaphore()

    @pl.loop(1, n)
    def _(i):
        pl.semaphore_signal(
            barrier, inc=1, device_id={"mode": lax.rem(me + i, n)},
            device_id_type=pl.DeviceIdType.MESH,
        )

    @pl.loop(1, nf)
    def _(i):
        pl.semaphore_signal(
            barrier, inc=1, device_id={"freq": lax.rem(band + i, nf)},
            device_id_type=pl.DeviceIdType.MESH,
        )

    mode_number = me * modes + lax.broadcasted_iota(jnp.int32, (bins, modes), 1)
    row_number = lax.broadcasted_iota(jnp.int32, (bins, modes), 0)
    count = jnp.zeros((bins, modes), jnp.int32)
    for f in range(bins):
        count = jnp.where(row_number == f, counts[f], count)
    living = jnp.where(mode_number < count, 1.0, 0.0).astype(jnp.float32)

    @pl.loop(0, n)
    def _(k):
        for c in range(2):
            x = exc[pl.ds(k * cs, cs), c].astype(jnp.float32) * living[None]
            amp[0, k, me, :, c * half:(c + 1) * half] = (
                x.reshape(half, modes).T.astype(jnp.bfloat16)
            )

    pl.semaphore_wait(barrier, n - 1 + nf - 1)
    send_own(0, owner(jnp.int32(0)))
    if n > 1:
        send_own(0, owner(jnp.int32(1)))

    def widen(x):
        return jnp.broadcast_to(x[None], (cs, bins, modes)).reshape(half, modes).T

    def turn_by(g):
        angle = wavenumber[...] * steps[g].astype(jnp.float32)
        narrow[0] = living * jnp.cos(angle)
        narrow[1] = living * jnp.sin(angle)
        for c in range(2):
            factor[g, c] = widen(narrow[c])

    def table_block(j):
        f = j * bins + offset_bin + lax.broadcasted_iota(jnp.int32, (bins, LANES), 0)
        lane = lax.broadcasted_iota(jnp.int32, (bins, LANES), 1)
        unit = 2.0 * math.pi / NT
        fine = lax.rem(f * lane, NT).astype(jnp.float32) * unit
        coarse = lax.rem(f * (lane * LANES), NT).astype(jnp.float32) * unit
        cos_fine, sin_fine = jnp.cos(fine), jnp.sin(fine)
        cos_coarse, sin_coarse = jnp.cos(coarse), jnp.sin(coarse)
        row = pl.multiple_of(j * (2 * bins), 2 * bins)
        for a in range(NT // LANES):
            ca = cos_coarse[:, a:a + 1]
            sa = sin_coarse[:, a:a + 1]
            at = slice(a * LANES, (a + 1) * LANES)
            table[pl.ds(row, bins), at] = (ca * cos_fine - sa * sin_fine).astype(jnp.bfloat16)
            table[pl.ds(row + bins, bins), at] = (
                -(sa * cos_fine + ca * sin_fine)
            ).astype(jnp.bfloat16)

    width = min(256, modes)

    def forward(p, d):
        g, position = phase(p)
        k = owner(position)
        for sign in (lead, -lead):
            @pl.when(
                jnp.logical_and(
                    jnp.logical_and(p < phases, wanted(g, me)),
                    jnp.logical_and(inside(me - sign * (d + 1)), wanted(g, me + sign)),
                )
            )
            def _(sign=sign):
                arrival(g, k, sign, d).wait_recv()
                hop(g, k, sign, d + 1).start()

    tiles = modes // width

    def couple(source, turn, g, k, shard, tile):
        rows = slice(tile * width, (tile + 1) * width)
        a = amp[g, k].reshape(n * modes, 2 * half)
        c = source[:, rows, :].reshape(2 * width, n * modes)
        product = jnp.dot(c, a, preferred_element_type=jnp.float32)
        by_real, by_imag = product[:width], product[width:]
        real = by_real[:, :half] - by_imag[:, half:]
        imag = by_real[:, half:] + by_imag[:, :half]
        fr, fi = turn[0, rows], turn[1, rows]
        amp[g + 1, k, shard, rows, 0:half] = (real * fr - imag * fi).astype(jnp.bfloat16)
        amp[g + 1, k, shard, rows, half:2 * half] = (real * fi + imag * fr).astype(jnp.bfloat16)

    turn_by(0)
    if n > 2:
        forward(jnp.int32(0), 0)
    for g in range(1, segments):
        turn_by(g)

    @pl.when(edge)
    def _():
        lend_factor().start()
        load(last).wait()

    for d in range(1, n - 2):
        forward(jnp.int32(0), d)

    @pl.loop(0, phases)
    def _(p):
        g, position = phase(p)
        k = owner(position)
        active = wanted(g, me)
        helping = jnp.logical_and(g == last, helper)

        @pl.when(jnp.logical_and(g == 0, position + 2 < n))
        def _():
            send_own(0, owner(position + 2))

        if relieve:
            @pl.when(jnp.logical_and(edge, p < lending))
            def _():
                @pl.loop(p * pieces // lending, (p + 1) * pieces // lending)
                def _(q):
                    lend(q).start()

        if n > 2:
            forward(p + 1, 0)

        for d in range(n - 1):
            for sign in (lead, -lead):
                @pl.when(
                    jnp.logical_and(
                        jnp.logical_and(active, inside(me - sign * (d + 1))),
                        jnp.logical_not(wanted(g, me + sign)),
                    )
                )
                def _(sign=sign, d=d):
                    arrival(g, k, sign, d).wait_recv()

        @pl.when(jnp.logical_and(position == 0, active))
        def _():
            load(g).wait()

        for tile in range(tiles):
            @pl.when(active)
            def _(tile=tile):
                couple(matrix.at[g], factor.at[g], g, k, me, tile)

            if tile + 1 < n - 2:
                forward(p + 1, tile + 1)
        for d in range(tiles + 1, n - 2):
            forward(p + 1, d)

        @pl.when(g < last)
        def _():
            send_own(g + 1, k)

        if relieve:
            @pl.when(helping)
            def _():
                @pl.when(position == 0)
                def _():
                    lend_factor().wait_recv()
                    for c in range(2):
                        lent_factor[c] = widen(lent_narrow[c])

                    @pl.loop(0, pieces)
                    def _(q):
                        lend(q).wait_recv()

                for tile in range(tiles):
                    couple(lent, lent_factor, last, k, partner, tile)

        def field_of(shard):
            rows = pl.ds(pl.multiple_of(shard * modes, modes), modes)
            return lax.dot_general(
                shapes[0, rows, :], amp[segments, k, shard], (((0,), (0,)), ((), ())),
                preferred_element_type=jnp.float32,
            )

        @pl.when(jnp.logical_and(g == last, active))
        def _():
            mine[...] = field_of(me)

            if relieve:
                @pl.when(helper)
                def _():
                    mine[...] += field_of(partner)

            @pl.when(k != me)
            def _():
                part[0, k] = mine[...].astype(jnp.bfloat16)
                to_owner(k).start()

            @pl.when(k == me)
            def _():
                total[...] = mine[...]

        @pl.loop(0, (nf - p + phases - 1) // phases)
        def _(i):
            table_block(p + i * phases)

    @pl.when(edge)
    def _():
        total[...] = jnp.zeros_like(total)

    @pl.loop(1, n)
    def _(i):
        z = lax.rem(me + i, n)

        @pl.when(jnp.logical_not(at_end(z)))
        def _():
            pltpu.make_async_remote_copy(
                src_ref=part.at[0, z],
                dst_ref=part.at[1, z],
                send_sem=own_send.at[z],
                recv_sem=own_recv.at[z],
                device_id={"mode": z},
                device_id_type=pl.DeviceIdType.MESH,
            ).wait_recv()
            total[...] += part[1, z].astype(jnp.float32)

    def weight(c):
        f_number = lax.rem(lax.broadcasted_iota(jnp.int32, (8, half), 1), bins)
        value = jnp.zeros((8, half), jnp.float32)
        for f in range(bins):
            value = jnp.where(f_number == f, spectrum[c, f], value)
        return value[0:1]

    wr, wi = weight(0), weight(1)
    fr, fi = total[:, 0:half], total[:, half:2 * half]
    weighted[0] = (wr * fr - wi * fi).astype(jnp.bfloat16)
    weighted[1] = (wr * fi + wi * fr).astype(jnp.bfloat16)

    def to_receiver(j, slot):
        return pltpu.make_async_remote_copy(
            src_ref=weighted.at[:, pl.ds(pl.multiple_of(j * rh, rh), rh)],
            dst_ref=landed.at[slot],
            send_sem=out_send.at[j],
            recv_sem=out_recv.at[slot],
            device_id={"freq": j},
            device_id_type=pl.DeviceIdType.MESH,
        )

    @pl.loop(1, nf)
    def _(i):
        to_receiver(lax.rem(band + i, nf), band).start()

    received[band] = weighted[:, pl.ds(pl.multiple_of(band * rh, rh), rh), :]

    @pl.loop(1, nf)
    def _(i):
        j = lax.rem(band + i, nf)
        to_receiver(j, j).wait_recv()
        received[j] = landed[j]

    @pl.loop(1, nf)
    def _(i):
        to_receiver(lax.rem(band + i, nf), band).wait_send()

    @pl.loop(0, phases)
    def _(p):
        g = p // n
        k = lax.rem(p, n)
        for d in range(n - 1):
            for sign in (lead, -lead):
                @pl.when(jnp.logical_and(inside(me - sign * d), wanted(g, me + sign)))
                def _(sign=sign, d=d):
                    hop(g, k, sign, d).wait_send()

    @pl.loop(1, n)
    def _(i):
        k = lax.rem(me + i, n)

        @pl.when(jnp.logical_not(edge))
        def _():
            to_owner(k).wait_send()

    if relieve:
        @pl.when(edge)
        def _():
            lend_factor().wait_send()

            @pl.loop(0, pieces)
            def _(q):
                lend(q).wait_send()


def shards(excitation, coupling, wavenumber, mode_counts, seg_steps, shapes, spectrum):
    n = lax.axis_size("mode")
    nf = lax.axis_size("freq")
    sources, _, bins, modes = excitation.shape
    segments, _, _, _, all_modes = coupling.shape
    receivers = shapes.shape[-1]
    cs = sources // n
    half = cs * bins
    rh = receivers // nf
    all_bins = bins * nf
    vmem = pl.BlockSpec(memory_space=pltpu.VMEM)
    smem = pl.BlockSpec(memory_space=pltpu.SMEM)
    dma = pltpu.SemaphoreType.DMA
    table, received = pl.pallas_call(
        functools.partial(propagate, n, nf, all_bins // 16),
        out_shape=(
            jax.ShapeDtypeStruct((nf * 2 * bins, NT), jnp.bfloat16),
            jax.ShapeDtypeStruct((nf, 2, rh, half), jnp.bfloat16),
        ),
        in_specs=[
            vmem, pl.BlockSpec(memory_space=pl.ANY), vmem, smem, smem, vmem, smem,
        ],
        out_specs=(vmem, vmem),
        scratch_shapes=[
            pltpu.VMEM((segments, 2, modes, all_modes), jnp.bfloat16),
            pltpu.VMEM((segments + 1, n, n, modes, 2 * half), jnp.bfloat16),
            pltpu.VMEM((segments, 2, modes, half), jnp.float32),
            pltpu.VMEM((2, receivers, half), jnp.bfloat16),
            pltpu.VMEM((nf, 2, rh, half), jnp.bfloat16),
            pltpu.VMEM((2, modes, all_modes), jnp.bfloat16),
            pltpu.VMEM((2, bins, modes), jnp.float32),
            pltpu.VMEM((2, bins, modes), jnp.float32),
            pltpu.VMEM((2, modes, half), jnp.float32),
            pltpu.VMEM((2, n, receivers, 2 * half), jnp.bfloat16),
            pltpu.VMEM((receivers, 2 * half), jnp.float32),
            pltpu.VMEM((receivers, 2 * half), jnp.float32),
            dma((segments,)),
            dma((segments, n, 2, n - 1)),
            dma((segments, n, 2, n - 1)),
            dma((n,)),
            dma((n,)),
            dma((nf,)),
            dma((nf,)),
            dma((max(segments - 1, 1) * n,)),
            dma((max(segments - 1, 1) * n,)),
            dma((2,)),
        ],
        compiler_params=pltpu.CompilerParams(
            collective_id=0, has_side_effects=True, vmem_limit_bytes=60 * 1024 * 1024
        ),
        name="propagate",
    )(
        excitation, coupling, wavenumber, mode_counts, seg_steps, shapes, spectrum,
    )
    left = received.reshape(nf, 2, rh, cs, bins).transpose(3, 2, 0, 1, 4)
    left = left.reshape(cs, rh, nf * 2 * bins)
    summed = lax.dot_general(
        left, table, (((2,), (0,)), ((), ())), preferred_element_type=jnp.float32
    )
    return summed * (1.0 / math.sqrt(all_bins))


def solution(mesh):
    in_specs = (
        P(None, None, "freq", "mode"),
        P(None, "freq", None, "mode", None),
        P("freq", "mode"),
        P("freq"),
        P(),
        P("freq", None, None),
        P(None, "freq"),
    )
    out_specs = P("mode", "freq", None)
    return jax.shard_map(shards, mesh=mesh, in_specs=in_specs, out_specs=out_specs, check_vma=False)
```

```python
import functools
import math

import jax
import jax.numpy as jnp
from jax import lax
from jax.experimental import pallas as pl
from jax.experimental.pallas import tpu as pltpu
from jax.sharding import PartitionSpec as P

NT = 4096
LANES = 128


def phase_order(segments, n):
    def key(pair):
        g, position = pair
        return (position + g * 0.625 * n, g)

    return sorted([(g, position) for g in range(segments) for position in range(n)], key=key)


def propagate(
    n, nf, offset_bin, exc, coupling, wavenumber, counts, steps, shapes, spectrum,
    table, received,
    matrix, amp, factor, weighted, landed, lent, lent_narrow, narrow, lent_factor, part, mine, total,
    load_sem, send_sem, recv_sem, own_send, own_recv, out_send, out_recv,
    lend_send, lend_recv, lend_factor_sem,
):
    segments = coupling.shape[0]
    sources, _, bins, modes = exc.shape
    cs = sources // n
    half = cs * bins
    receivers = shapes.shape[-1]
    rh = receivers // nf
    phases = segments * n
    me = lax.axis_index("mode")
    band = lax.axis_index("freq")

    relieve = n >= 4 and segments >= 2
    last = segments - 1
    order = phase_order(segments, n)
    first_last = [g for g, _ in order].index(last)
    lending = max(first_last - 1, 1)
    pieces = max(last, 1) * n
    piece = modes // pieces

    def at_end(z):
        return jnp.logical_and(relieve, jnp.logical_or(z == 0, z == n - 1))

    edge = at_end(me)
    helper = jnp.logical_and(relieve, jnp.logical_or(me == 1, me == n - 2))
    partner = jnp.where(me == 1, 0, n - 1)
    inward = jnp.where(me == 0, min(1, n - 1), max(n - 2, 0))

    def owner(position):
        return jnp.where(
            lax.rem(position, 2) == 0, position // 2, n - 1 - position // 2
        )

    def phase(p):
        g, position = jnp.int32(0), jnp.int32(0)
        for i, (at_g, at_position) in enumerate(order):
            g = jnp.where(p == i, at_g, g)
            position = jnp.where(p == i, at_position, position)
        return g, position

    def lend(q):
        rows = pl.ds(pl.multiple_of(q * piece, piece), piece)
        return pltpu.make_async_remote_copy(
            src_ref=matrix.at[last, :, rows],
            dst_ref=lent.at[:, rows],
            send_sem=lend_send.at[q],
            recv_sem=lend_recv.at[q],
            device_id={"mode": inward},
            device_id_type=pl.DeviceIdType.MESH,
        )

    def lend_factor():
        return pltpu.make_async_remote_copy(
            src_ref=narrow,
            dst_ref=lent_narrow,
            send_sem=lend_factor_sem.at[0],
            recv_sem=lend_factor_sem.at[1],
            device_id={"mode": inward},
            device_id_type=pl.DeviceIdType.MESH,
        )

    def load(g):
        return pltpu.make_async_copy(coupling.at[g, 0], matrix.at[g], load_sem.at[g])

    def hop(g, k, sign, d):
        shard = me - sign * d
        way = (sign + 1) // 2
        return pltpu.make_async_remote_copy(
            src_ref=amp.at[g, k, shard],
            dst_ref=amp.at[g, k, shard],
            send_sem=send_sem.at[g, k, way, d],
            recv_sem=recv_sem.at[g, k, way, d],
            device_id={"mode": me + sign},
            device_id_type=pl.DeviceIdType.MESH,
        )

    def arrival(g, k, sign, d):
        shard = me - sign * (d + 1)
        way = (sign + 1) // 2
        return pltpu.make_async_remote_copy(
            src_ref=amp.at[g, k, shard],
            dst_ref=amp.at[g, k, shard],
            send_sem=send_sem.at[g, k, way, d],
            recv_sem=recv_sem.at[g, k, way, d],
            device_id={"mode": me - sign},
            device_id_type=pl.DeviceIdType.MESH,
        )

    def inside(z):
        return jnp.logical_and(z >= 0, z < n)

    lead = jnp.where(me < n // 2, -1, 1)

    def wanted(g, z):
        return jnp.logical_and(inside(z), jnp.logical_not(jnp.logical_and(g == last, at_end(z))))

    def send_own(g, k):
        for sign in (lead, -lead):
            @pl.when(wanted(g, me + sign))
            def _(sign=sign):
                hop(g, k, sign, 0).start()

    def to_owner(k):
        return pltpu.make_async_remote_copy(
            src_ref=part.at[0, k],
            dst_ref=part.at[1, me],
            send_sem=own_send.at[k],
            recv_sem=own_recv.at[me],
            device_id={"mode": k},
            device_id_type=pl.DeviceIdType.MESH,
        )

    for g in range(segments):
        load(g).start()

    barrier = pltpu.get_barrier_semaphore()

    @pl.loop(1, n)
    def _(i):
        pl.semaphore_signal(
            barrier, inc=1, device_id={"mode": lax.rem(me + i, n)},
            device_id_type=pl.DeviceIdType.MESH,
        )

    @pl.loop(1, nf)
    def _(i):
        pl.semaphore_signal(
            barrier, inc=1, device_id={"freq": lax.rem(band + i, nf)},
            device_id_type=pl.DeviceIdType.MESH,
        )

    mode_number = me * modes + lax.broadcasted_iota(jnp.int32, (bins, modes), 1)
    row_number = lax.broadcasted_iota(jnp.int32, (bins, modes), 0)
    count = jnp.zeros((bins, modes), jnp.int32)
    for f in range(bins):
        count = jnp.where(row_number == f, counts[f], count)
    living = jnp.where(mode_number < count, 1.0, 0.0).astype(jnp.float32)

    @pl.loop(0, n)
    def _(k):
        for c in range(2):
            x = exc[pl.ds(k * cs, cs), c].astype(jnp.float32) * living[None]
            amp[0, k, me, :, c * half:(c + 1) * half] = (
                x.reshape(half, modes).T.astype(jnp.bfloat16)
            )

    pl.semaphore_wait(barrier, n - 1 + nf - 1)
    send_own(0, owner(jnp.int32(0)))
    if n > 1:
        send_own(0, owner(jnp.int32(1)))

    def widen(x):
        return jnp.broadcast_to(x[None], (cs, bins, modes)).reshape(half, modes).T

    def turn_by(g):
        angle = wavenumber[...] * steps[g].astype(jnp.float32)
        narrow[0] = living * jnp.cos(angle)
        narrow[1] = living * jnp.sin(angle)
        for c in range(2):
            factor[g, c] = widen(narrow[c])

    def table_block(j):
        f = j * bins + offset_bin + lax.broadcasted_iota(jnp.int32, (bins, LANES), 0)
        lane = lax.broadcasted_iota(jnp.int32, (bins, LANES), 1)
        unit = 2.0 * math.pi / NT
        fine = lax.rem(f * lane, NT).astype(jnp.float32) * unit
        coarse = lax.rem(f * (lane * LANES), NT).astype(jnp.float32) * unit
        cos_fine, sin_fine = jnp.cos(fine), jnp.sin(fine)
        cos_coarse, sin_coarse = jnp.cos(coarse), jnp.sin(coarse)
        row = pl.multiple_of(j * (2 * bins), 2 * bins)
        for a in range(NT // LANES):
            ca = cos_coarse[:, a:a + 1]
            sa = sin_coarse[:, a:a + 1]
            at = slice(a * LANES, (a + 1) * LANES)
            table[pl.ds(row, bins), at] = (ca * cos_fine - sa * sin_fine).astype(jnp.bfloat16)
            table[pl.ds(row + bins, bins), at] = (
                -(sa * cos_fine + ca * sin_fine)
            ).astype(jnp.bfloat16)

    width = min(256, modes)

    def forward(p, d):
        g, position = phase(p)
        k = owner(position)
        for sign in (lead, -lead):
            @pl.when(
                jnp.logical_and(
                    jnp.logical_and(p < phases, wanted(g, me)),
                    jnp.logical_and(inside(me - sign * (d + 1)), wanted(g, me + sign)),
                )
            )
            def _(sign=sign):
                arrival(g, k, sign, d).wait_recv()
                hop(g, k, sign, d + 1).start()

    tiles = modes // width

    def couple(source, turn, g, k, shard, tile):
        rows = slice(tile * width, (tile + 1) * width)
        a = amp[g, k].reshape(n * modes, 2 * half)
        c = source[:, rows, :].reshape(2 * width, n * modes)
        product = jnp.dot(c, a, preferred_element_type=jnp.float32)
        by_real, by_imag = product[:width], product[width:]
        real = by_real[:, :half] - by_imag[:, half:]
        imag = by_real[:, half:] + by_imag[:, :half]
        fr, fi = turn[0, rows], turn[1, rows]
        amp[g + 1, k, shard, rows, 0:half] = (real * fr - imag * fi).astype(jnp.bfloat16)
        amp[g + 1, k, shard, rows, half:2 * half] = (real * fi + imag * fr).astype(jnp.bfloat16)

    turn_by(0)
    if n > 2:
        forward(jnp.int32(0), 0)
    for g in range(1, segments):
        turn_by(g)

    @pl.when(edge)
    def _():
        lend_factor().start()
        load(last).wait()

    for d in range(1, n - 2):
        forward(jnp.int32(0), d)
    if n > 2:
        forward(jnp.int32(1), 0)

    @pl.loop(0, phases)
    def _(p):
        g, position = phase(p)
        k = owner(position)
        active = wanted(g, me)
        helping = jnp.logical_and(g == last, helper)

        @pl.when(jnp.logical_and(g == 0, position + 2 < n))
        def _():
            send_own(0, owner(position + 2))

        if relieve:
            @pl.when(jnp.logical_and(edge, p < lending))
            def _():
                @pl.loop(p * pieces // lending, (p + 1) * pieces // lending)
                def _(q):
                    lend(q).start()

        if n > 2:
            forward(p + 2, 0)
        if n > 3:
            forward(p + 1, 1)

        for d in range(n - 1):
            for sign in (lead, -lead):
                @pl.when(
                    jnp.logical_and(
                        jnp.logical_and(active, inside(me - sign * (d + 1))),
                        jnp.logical_not(wanted(g, me + sign)),
                    )
                )
                def _(sign=sign, d=d):
                    arrival(g, k, sign, d).wait_recv()

        @pl.when(jnp.logical_and(position == 0, active))
        def _():
            load(g).wait()

        for tile in range(tiles):
            @pl.when(active)
            def _(tile=tile):
                couple(matrix.at[g], factor.at[g], g, k, me, tile)

            if tile + 2 < n - 2:
                forward(p + 1, tile + 2)
        for d in range(tiles + 2, n - 2):
            forward(p + 1, d)

        @pl.when(g < last)
        def _():
            send_own(g + 1, k)

        if relieve:
            @pl.when(helping)
            def _():
                @pl.when(position == 0)
                def _():
                    lend_factor().wait_recv()
                    for c in range(2):
                        lent_factor[c] = widen(lent_narrow[c])

                    @pl.loop(0, pieces)
                    def _(q):
                        lend(q).wait_recv()

                for tile in range(tiles):
                    couple(lent, lent_factor, last, k, partner, tile)

        def field_of(shard):
            rows = pl.ds(pl.multiple_of(shard * modes, modes), modes)
            return lax.dot_general(
                shapes[0, rows, :], amp[segments, k, shard], (((0,), (0,)), ((), ())),
                preferred_element_type=jnp.float32,
            )

        @pl.when(jnp.logical_and(g == last, active))
        def _():
            mine[...] = field_of(me)

            if relieve:
                @pl.when(helper)
                def _():
                    mine[...] += field_of(partner)

            @pl.when(k != me)
            def _():
                part[0, k] = mine[...].astype(jnp.bfloat16)
                to_owner(k).start()

            @pl.when(k == me)
            def _():
                total[...] = mine[...]

        @pl.loop(0, (nf - p + phases - 1) // phases)
        def _(i):
            table_block(p + i * phases)

    @pl.when(edge)
    def _():
        total[...] = jnp.zeros_like(total)

    @pl.loop(1, n)
    def _(i):
        z = lax.rem(me + i, n)

        @pl.when(jnp.logical_not(at_end(z)))
        def _():
            pltpu.make_async_remote_copy(
                src_ref=part.at[0, z],
                dst_ref=part.at[1, z],
                send_sem=own_send.at[z],
                recv_sem=own_recv.at[z],
                device_id={"mode": z},
                device_id_type=pl.DeviceIdType.MESH,
            ).wait_recv()
            total[...] += part[1, z].astype(jnp.float32)

    def weight(c):
        f_number = lax.rem(lax.broadcasted_iota(jnp.int32, (8, half), 1), bins)
        value = jnp.zeros((8, half), jnp.float32)
        for f in range(bins):
            value = jnp.where(f_number == f, spectrum[c, f], value)
        return value[0:1]

    wr, wi = weight(0), weight(1)
    fr, fi = total[:, 0:half], total[:, half:2 * half]
    weighted[0] = (wr * fr - wi * fi).astype(jnp.bfloat16)
    weighted[1] = (wr * fi + wi * fr).astype(jnp.bfloat16)

    def to_receiver(j, slot):
        return pltpu.make_async_remote_copy(
            src_ref=weighted.at[:, pl.ds(pl.multiple_of(j * rh, rh), rh)],
            dst_ref=landed.at[slot],
            send_sem=out_send.at[j],
            recv_sem=out_recv.at[slot],
            device_id={"freq": j},
            device_id_type=pl.DeviceIdType.MESH,
        )

    @pl.loop(1, nf)
    def _(i):
        to_receiver(lax.rem(band + i, nf), band).start()

    received[band] = weighted[:, pl.ds(pl.multiple_of(band * rh, rh), rh), :]

    @pl.loop(1, nf)
    def _(i):
        j = lax.rem(band + i, nf)
        to_receiver(j, j).wait_recv()
        received[j] = landed[j]

    @pl.loop(1, nf)
    def _(i):
        to_receiver(lax.rem(band + i, nf), band).wait_send()

    @pl.loop(0, phases)
    def _(p):
        g = p // n
        k = lax.rem(p, n)
        for d in range(n - 1):
            for sign in (lead, -lead):
                @pl.when(jnp.logical_and(inside(me - sign * d), wanted(g, me + sign)))
                def _(sign=sign, d=d):
                    hop(g, k, sign, d).wait_send()

    @pl.loop(1, n)
    def _(i):
        k = lax.rem(me + i, n)

        @pl.when(jnp.logical_not(edge))
        def _():
            to_owner(k).wait_send()

    if relieve:
        @pl.when(edge)
        def _():
            lend_factor().wait_send()

            @pl.loop(0, pieces)
            def _(q):
                lend(q).wait_send()


def shards(excitation, coupling, wavenumber, mode_counts, seg_steps, shapes, spectrum):
    n = lax.axis_size("mode")
    nf = lax.axis_size("freq")
    sources, _, bins, modes = excitation.shape
    segments, _, _, _, all_modes = coupling.shape
    receivers = shapes.shape[-1]
    cs = sources // n
    half = cs * bins
    rh = receivers // nf
    all_bins = bins * nf
    vmem = pl.BlockSpec(memory_space=pltpu.VMEM)
    smem = pl.BlockSpec(memory_space=pltpu.SMEM)
    dma = pltpu.SemaphoreType.DMA
    table, received = pl.pallas_call(
        functools.partial(propagate, n, nf, all_bins // 16),
        out_shape=(
            jax.ShapeDtypeStruct((nf * 2 * bins, NT), jnp.bfloat16),
            jax.ShapeDtypeStruct((nf, 2, rh, half), jnp.bfloat16),
        ),
        in_specs=[
            vmem, pl.BlockSpec(memory_space=pl.ANY), vmem, smem, smem, vmem, smem,
        ],
        out_specs=(vmem, vmem),
        scratch_shapes=[
            pltpu.VMEM((segments, 2, modes, all_modes), jnp.bfloat16),
            pltpu.VMEM((segments + 1, n, n, modes, 2 * half), jnp.bfloat16),
            pltpu.VMEM((segments, 2, modes, half), jnp.float32),
            pltpu.VMEM((2, receivers, half), jnp.bfloat16),
            pltpu.VMEM((nf, 2, rh, half), jnp.bfloat16),
            pltpu.VMEM((2, modes, all_modes), jnp.bfloat16),
            pltpu.VMEM((2, bins, modes), jnp.float32),
            pltpu.VMEM((2, bins, modes), jnp.float32),
            pltpu.VMEM((2, modes, half), jnp.float32),
            pltpu.VMEM((2, n, receivers, 2 * half), jnp.bfloat16),
            pltpu.VMEM((receivers, 2 * half), jnp.float32),
            pltpu.VMEM((receivers, 2 * half), jnp.float32),
            dma((segments,)),
            dma((segments, n, 2, n - 1)),
            dma((segments, n, 2, n - 1)),
            dma((n,)),
            dma((n,)),
            dma((nf,)),
            dma((nf,)),
            dma((max(segments - 1, 1) * n,)),
            dma((max(segments - 1, 1) * n,)),
            dma((2,)),
        ],
        compiler_params=pltpu.CompilerParams(
            collective_id=0, has_side_effects=True, vmem_limit_bytes=60 * 1024 * 1024
        ),
        name="propagate",
    )(
        excitation, coupling, wavenumber, mode_counts, seg_steps, shapes, spectrum,
    )
    left = received.reshape(nf, 2, rh, cs, bins).transpose(3, 2, 0, 1, 4)
    left = left.reshape(cs, rh, nf * 2 * bins)
    summed = lax.dot_general(
        left, table, (((2,), (0,)), ((), ())), preferred_element_type=jnp.float32
    )
    return summed * (1.0 / math.sqrt(all_bins))


def solution(mesh):
    in_specs = (
        P(None, None, "freq", "mode"),
        P(None, "freq", None, "mode", None),
        P("freq", "mode"),
        P("freq"),
        P(),
        P("freq", None, None),
        P(None, "freq"),
    )
    out_specs = P("mode", "freq", None)
    return jax.shard_map(shards, mesh=mesh, in_specs=in_specs, out_specs=out_specs, check_vma=False)
```
